128 devices in a mesh: tx: 8 (over x, core), ty: 16 (over z, y).
Axes of the slice: x: 4, y: 4, z: 4, core: 2. Of those that a mesh axis runs over, the one named last changes fastest.
Arguments:
- right_side: bfloat16 [524288, 512], P(('tx', 'ty')), may hold values from -6 to 6
- points: bfloat16 [8, 524288], P(None, ('tx', 'ty'))
- leaf_inverse: bfloat16 [2048, 256, 256], P(('tx', 'ty'))
- level_one: bfloat16 [256, 1024, 1024], P(('tx', 'ty'))
- second_level_coupling: bfloat16 [16, 2048, 2048], P('ty', 'tx')
- neighbours: int32 [2048, 8], P(('tx', 'ty')), may hold values from 0 to 2047, as said below
- counts: int32 [2048], P(('tx', 'ty')), may hold values from 1 to 8
- leaf_skeleton: int32 [2048, 128], P(('tx', 'ty')), may hold values from 0 to 255, as said below
- node_skeleton: int32 [256, 128], P(('tx', 'ty')), may hold values from 0 to 1023, as said below
Outputs:
- solution: float32 [524288, 512], P(('tx', 'ty'))
The draws below stay inside these ranges and needn't reach their ends.
Inputs may be any that keep to these rules, and one draw needn't show every extreme that they name: Each leaf's neighbours are distinct leaves other than itself, in the same block of 256 consecutive leaves, within 8 leaves of it; slot 0 lies exactly 8 leaves away. `leaf_skeleton`: distinct within each leaf. `node_skeleton`: distinct within each node.
All inputs are finite; a program needn't handle non-finite values.
Results may differ from the reference program's by a relative error of at most 0.009.
Values may be sent and summed in bfloat16 or wider, within the bound.
A program may use at most 320 MiB of HBM per device.

```python
import math
import jax
import jax.numpy as jnp
from jax import lax

P_SIZE = 256
DIM = 8
SK = 128
GROUP = 8
LEAF_DEV = 16
NBR = 8
WIN = 8
R = 512
LEAVES = 2048
POINTS = 524288
ROW_LEAVES = 256
NODE_DEV = 2
NODES1 = 256
NODES2 = 16
ORDER2 = 2048
N_TX = 8
N_TY = 16


def dominant_matrix(noise, order, spread):
    return jnp.eye(order, dtype=jnp.float32) + noise * (spread / math.sqrt(order))


def distinct_rows(key, rows, choices, take):
    scores = jax.random.randint(key, (rows, choices), 0, 2 ** 19, dtype=jnp.int32) * 1024 + jnp.arange(choices, dtype=jnp.int32)[None, :]
    picked = lax.top_k(scores, take)[1]
    return picked.astype(jnp.int32)


def trajectory_points(key, amplitude, jitter):
    blocks = LEAVES // ROW_LEAVES
    key_freq, key_phase, key_place = jax.random.split(key, 3)
    freq = jax.random.uniform(key_freq, (DIM, blocks, 1, 1), jnp.float32, 0.06, 0.16)
    phase = jax.random.uniform(key_phase, (DIM, blocks, 1, 1), jnp.float32, -math.pi, math.pi)
    reach = WIN // 2 + 1
    along = jnp.arange(ROW_LEAVES, dtype=jnp.float32)[None, None, :, None] + reach * jax.random.uniform(key_place, (1, blocks, ROW_LEAVES, P_SIZE), jnp.float32, -1.0, 1.0)
    return (amplitude * jnp.sin(freq * along + phase) + jitter).reshape(DIM, POINTS)


def draw_points(key, part):
    key = jax.random.fold_in(key, 17)
    key_path, key_jitter = jax.random.split(key)
    shape = (DIM, LEAVES // ROW_LEAVES, ROW_LEAVES, P_SIZE)
    jitter = jax.random.normal(key_jitter, shape, jnp.float32) * 1.4
    coords = trajectory_points(key_path, 12.0, jitter)
    return coords.astype(jnp.bfloat16)


def draw_leaf_inverse(key, part):
    key = jax.random.fold_in(key, 11)
    shape = (LEAVES, P_SIZE, P_SIZE)
    noise = jax.random.normal(key, shape, jnp.float32)
    return dominant_matrix(noise, P_SIZE, 0.5).astype(jnp.bfloat16)


def draw_level_one(key, part):
    key = jax.random.fold_in(key, 12)
    shape = (NODES1, GROUP * SK, GROUP * SK)
    noise = jax.random.normal(key, shape, jnp.float32)
    return dominant_matrix(noise, GROUP * SK, 0.7).astype(jnp.bfloat16)


def draw_second_level_coupling(key, part):
    key = jax.random.fold_in(key, 13)
    shape = (NODES2, ORDER2, ORDER2)
    noise = jax.random.normal(key, shape, jnp.float32)
    return dominant_matrix(noise, ORDER2, 1.0).astype(jnp.bfloat16)


def draw_neighbours(key, part):
    key = jax.random.fold_in(key, 14)
    leaf_ids = jnp.arange(LEAVES, dtype=jnp.int32)
    row_pos = leaf_ids % ROW_LEAVES
    offsets = jnp.concatenate([jnp.arange(-WIN, 0, dtype=jnp.int32), jnp.arange(1, WIN + 1, dtype=jnp.int32)])
    landing = row_pos[:, None] + offsets[None, :]
    valid = (landing >= 0) & (landing < ROW_LEAVES)
    scores = jax.random.randint(key, (LEAVES, 2 * WIN), 0, 2 ** 20, dtype=jnp.int32) * 64 + jnp.arange(2 * WIN, dtype=jnp.int32)[None, :]
    plus_ok = row_pos + WIN < ROW_LEAVES
    favored = jnp.where(plus_ok[:, None], offsets[None, :] == WIN, offsets[None, :] == -WIN)
    scores = jnp.where(favored, scores + 2 ** 27, scores)
    scores = jnp.where(valid, scores, -1 - jnp.arange(2 * WIN, dtype=jnp.int32)[None, :])
    picked = lax.top_k(scores, NBR)[1]
    return (leaf_ids[:, None] + offsets[picked]).astype(jnp.int32)


def draw_leaf_skeleton(key, part):
    key = jax.random.fold_in(key, 15)
    return distinct_rows(key, LEAVES, P_SIZE, SK)


def draw_node_skeleton(key, part):
    key = jax.random.fold_in(key, 16)
    return distinct_rows(key, NODES1, GROUP * SK, SK)


def set_ends(entries, rng, least, top_value):
    longest = entries.shape.index(max(entries.shape))
    spots = []
    for shift in (0, 1):
        where = [jax.random.randint(jax.random.fold_in(rng, axis), (), 0, length) for axis, length in enumerate(entries.shape)]
        where[longest] = (where[longest] + shift) % entries.shape[longest]
        spots.append(tuple(where))
    return entries.at[spots[0]].set(least).at[spots[1]].set(top_value)


def levels(own_key, shape, cuts, least, top_value):
    loudness = 1.0
    for dim, parts in cuts:
        heights = jax.random.uniform(jax.random.fold_in(jax.random.fold_in(own_key, 6), dim), (parts,), jnp.float32, least / len(cuts), top_value / len(cuts))
        loudness = loudness * jnp.repeat(jnp.exp(heights), shape[dim] // parts).reshape((-1,) + (1,) * (len(shape) - 1 - dim))
    return loudness


def scatter_about(key, extent, deviation, limit, shards=(), held_as=jnp.bfloat16):
    loudness = levels(key, extent, shards, -0.22, 0.18) if shards else 1.0
    drawn = jax.random.normal(key, extent, jnp.float32) * deviation * loudness
    return jnp.minimum(jnp.maximum(drawn, -limit), limit).astype(held_as)


def setup_inputs(seed: int = 0) -> dict:
    keys = jax.random.split(jax.random.key(seed), 10)
    return {
        "right_side": scatter_about(keys[0], (POINTS, R), 1.0, 6.0, ((0, 128),)),
        "points": draw_points(jax.random.fold_in(keys[9], 71), 0),
        "leaf_inverse": draw_leaf_inverse(jax.random.fold_in(keys[9], 71), 0),
        "level_one": draw_level_one(jax.random.fold_in(keys[9], 71), 0),
        "second_level_coupling": draw_second_level_coupling(jax.random.fold_in(keys[9], 71), 0),
        "neighbours": draw_neighbours(jax.random.fold_in(keys[9], 71), 0),
        "counts": set_ends(jax.random.randint(keys[6], (LEAVES,), 1, NBR + 1), jax.random.fold_in(keys[6], 1), 1, NBR).astype(jnp.int32),
        "leaf_skeleton": draw_leaf_skeleton(jax.random.fold_in(keys[9], 71), 0),
        "node_skeleton": draw_node_skeleton(jax.random.fold_in(keys[9], 71), 0),
    }


def kernel_block(own, other):
    cross = jnp.einsum("ldi,ldj->lij", own, other)
    own_sq = jnp.sum(own * own, axis=1)[:, :, None]
    other_sq = jnp.sum(other * other, axis=1)[:, None, :]
    return jnp.exp(-(own_sq + other_sq - 2.0 * cross) * (0.5 / DIM))


def reference(right_side, points, leaf_inverse, level_one, second_level_coupling, neighbours, counts, leaf_skeleton, node_skeleton):
    nearfield_scale = P_SIZE ** -0.5
    coords = points.astype(jnp.float32).reshape(DIM, LEAVES, P_SIZE).transpose(1, 0, 2)
    rhs_all = right_side.reshape(LEAVES, P_SIZE, R)

    def near_rows(start):
        ids = start + jnp.arange(LEAF_DEV, dtype=jnp.int32)
        own = coords[ids]
        lists = neighbours[ids]
        live_count = counts[ids]
        total = jnp.zeros((LEAF_DEV, P_SIZE, R), jnp.float32)
        for slot in range(NBR):
            other = lists[:, slot]
            live = (slot < live_count).astype(jnp.float32)
            weights = (kernel_block(own, coords[other]) * live[:, None, None]).astype(jnp.bfloat16)
            total = total + jnp.einsum("lij,ljr->lir", weights.astype(jnp.float32), rhs_all[other].astype(jnp.float32), precision=lax.Precision.HIGHEST)
        return (rhs_all[ids].astype(jnp.float32) - total * nearfield_scale).astype(jnp.bfloat16)

    starts = jnp.arange(0, LEAVES, LEAF_DEV, dtype=jnp.int32)
    resid = lax.map(near_rows, starts).reshape(LEAVES, P_SIZE, R)
    inner = jnp.einsum("lij,ljr->lir", leaf_inverse.astype(jnp.float32), resid.astype(jnp.float32), precision=lax.Precision.HIGHEST)
    skel = jnp.take_along_axis(inner, leaf_skeleton[:, :, None], axis=1).astype(jnp.bfloat16)
    upward = skel.reshape(NODES1, GROUP * SK, R)
    top = jnp.take_along_axis(upward, node_skeleton[:, :, None], axis=1)
    stacked_blocks = top.reshape(N_TX, N_TY, NODE_DEV * SK, R).transpose(1, 0, 2, 3).reshape(N_TY, ORDER2, R)
    backward_sweep = jnp.einsum("bnd,bdx->bnx", second_level_coupling.astype(jnp.float32), stacked_blocks.astype(jnp.float32), precision=lax.Precision.HIGHEST)
    backward_sweep = backward_sweep.reshape(N_TY, N_TX, NODE_DEV * SK, R).transpose(1, 0, 2, 3).reshape(NODES1, SK, R)
    node_ids = jnp.arange(NODES1, dtype=jnp.int32)[:, None]
    downward = upward.astype(jnp.float32).at[node_ids, node_skeleton].add(-backward_sweep).astype(jnp.bfloat16)
    coupling_block = jnp.einsum("nij,njr->nir", level_one.astype(jnp.float32), downward.astype(jnp.float32), precision=lax.Precision.HIGHEST).astype(jnp.bfloat16)
    coupling_block = coupling_block.reshape(LEAVES, SK, R)
    column_entries = jnp.take_along_axis(leaf_inverse, leaf_skeleton[:, None, :], axis=2)
    woodbury_correction = jnp.einsum("wkd,wdb->wkb", column_entries.astype(jnp.float32), coupling_block.astype(jnp.float32), precision=lax.Precision.HIGHEST)
    return (inner - woodbury_correction).reshape(POINTS, R)
```

```python
import functools
import math

import jax
import jax.numpy as jnp
from jax import lax
from jax.experimental import pallas as pl
from jax.experimental.pallas import tpu as pltpu
from jax.sharding import PartitionSpec as P

PTS = 256
DIM = 8
SK = 128
GROUP = 8
NBR = 8
WIN = 8
MESH = pl.DeviceIdType.MESH
F32 = jnp.float32
BF16 = jnp.bfloat16
LOG2E = math.log2(math.e)


def mm(a, b):
    return jnp.dot(a, b, preferred_element_type=F32)


def device_kernel(
    dims,
    rhs,
    pts,
    leaf_inv,
    level_one,
    coupling,
    neigh,
    counts,
    leaf_skel,
    node_skel,
    out,
    *scratch,
):
    leaves, nodes, widths, n_tx, n_ty = dims
    chunks = len(widths)
    starts = [sum(widths[:c]) for c in range(chunks)]
    ext, up, gath, top, scratch = (
        scratch[:chunks],
        scratch[chunks : 2 * chunks],
        scratch[2 * chunks : 3 * chunks],
        scratch[3 * chunks : 4 * chunks],
        scratch[4 * chunks :],
    )
    (
        weights,
        inv,
        lone,
        coup_rows,
        inv_cols,
        leaf_pick,
        node_pick,
        node_spread,
        p_right,
        p_left,
        p_from_left,
        p_from_right,
        v_ext,
        u_all,
        u_leaf,
        halo_send,
        halo_recv,
        pts_send,
        pts_recv,
        top_send,
        top_recv,
        own_sem,
        load_sem,
    ) = scratch
    tx = lax.axis_index("tx")
    ty = lax.axis_index("ty")
    right = lax.rem(ty + 1, n_ty)
    left = lax.rem(ty + n_ty - 1, n_ty)
    own_rows = leaves * PTS
    side = WIN * PTS
    half = side // 2
    node_rows = GROUP * SK

    barrier = pltpu.get_barrier_semaphore()
    for t in (left, right):
        pl.semaphore_signal(barrier, inc=1, device_id=(tx, t), device_id_type=MESH)
    for k in range(1, n_tx):
        pl.semaphore_signal(
            barrier, inc=1, device_id=(lax.rem(tx + k, n_tx), ty), device_id_type=MESH
        )
    pl.semaphore_wait(barrier, 2 + n_tx - 1)

    def halo(c):
        cols = pl.ds(starts[c], widths[c])
        return (
            pltpu.make_async_remote_copy(
                src_ref=rhs.at[pl.ds(leaves - WIN, WIN), :, cols],
                dst_ref=ext[c].at[pl.ds(0, WIN)],
                send_sem=halo_send.at[c, 0],
                recv_sem=halo_recv.at[c, 0],
                device_id=(tx, right),
                device_id_type=MESH,
            ),
            pltpu.make_async_remote_copy(
                src_ref=rhs.at[pl.ds(0, WIN), :, cols],
                dst_ref=ext[c].at[pl.ds(WIN + leaves, WIN)],
                send_sem=halo_send.at[c, 1],
                recv_sem=halo_recv.at[c, 1],
                device_id=(tx, left),
                device_id_type=MESH,
            ),
        )

    def points_halo():
        return (
            pltpu.make_async_remote_copy(
                src_ref=p_right,
                dst_ref=p_from_left,
                send_sem=pts_send.at[0],
                recv_sem=pts_recv.at[0],
                device_id=(tx, right),
                device_id_type=MESH,
            ),
            pltpu.make_async_remote_copy(
                src_ref=p_left,
                dst_ref=p_from_right,
                send_sem=pts_send.at[1],
                recv_sem=pts_recv.at[1],
                device_id=(tx, left),
                device_id_type=MESH,
            ),
        )

    def own(c):
        return pltpu.make_async_copy(
            rhs.at[:, :, pl.ds(starts[c], widths[c])],
            ext[c].at[pl.ds(WIN, leaves)],
            own_sem.at[c],
        )

    loads = (
        pltpu.make_async_copy(leaf_inv, inv, load_sem.at[0]),
        pltpu.make_async_copy(coupling.at[0], coup_rows, load_sem.at[1]),
        pltpu.make_async_copy(level_one, lone, load_sem.at[2]),
    )

    coords = pts[...].astype(F32)

    def two_rows(x):
        return jnp.concatenate([x[:, :half], x[:, half:]], axis=0).astype(BF16)

    p_right[...] = two_rows(coords[:, own_rows - side :])
    p_left[...] = two_rows(coords[:, :side])
    for copy in points_halo():
        copy.start()
    for c in range(chunks):
        for copy in halo(c):
            copy.start()
    for copy in loads:
        copy.start()
    for c in range(chunks):
        own(c).start()

    def tails(x, sign_rows):
        sq = jnp.sum(x * x, axis=0, keepdims=True) * (-0.5 / DIM)
        high = sq.astype(BF16).astype(F32)
        rest = sq - high
        mid = rest.astype(BF16).astype(F32)
        low = rest - mid
        row = lax.broadcasted_iota(jnp.int32, (8, x.shape[1]), 0)
        at = 3 * sign_rows
        parts = jnp.where(
            row == at, high, jnp.where(row == at + 1, mid, jnp.where(row == at + 2, low, 1.0))
        )
        return jnp.where(row < 6, parts, 0.0)

    def put_other(place, x):
        block = jnp.concatenate([x, tails(x, 0)], axis=0).astype(BF16)
        for j in range(x.shape[1] // PTS):
            v_ext[place + j] = block[:, j * PTS : (j + 1) * PTS]

    u_all[...] = jnp.concatenate([coords * (1.0 / DIM), tails(coords, 1)], axis=0)
    put_other(WIN, coords)

    loads[0].wait()

    def leaf_setup(i, _):
        rows = pl.ds(pl.multiple_of(i * PTS, PTS), PTS)
        u_leaf[i] = u_all[:, rows].T.astype(BF16)
        spot = lax.broadcasted_iota(jnp.int32, (PTS, SK), 0)
        spread = (spot == leaf_skel[pl.ds(i, 1), :]).astype(F32)
        leaf_pick[i] = spread.T.astype(BF16)
        inv_cols[i] = mm(inv[i], spread.astype(BF16)).astype(BF16)
        return 0

    lax.fori_loop(0, leaves, leaf_setup, 0)
    for n in range(nodes):
        spot = lax.broadcasted_iota(jnp.int32, (node_rows, SK), 0)
        spread = (spot == node_skel[pl.ds(n, 1), :]).astype(F32)
        node_spread[n] = spread.astype(BF16)
        node_pick[n] = spread.T.astype(BF16)

    for copy in points_halo():
        copy.wait()
    for block, place in ((p_from_left, 0), (p_from_right, WIN + leaves)):
        far = block[...].astype(F32)
        put_other(place, far[:DIM])
        put_other(place + WIN // 2, far[DIM:])

    base = (tx * n_ty + ty) * leaves - WIN

    def place_of(i, s):
        return jnp.clip(neigh[s, i] - base, 0, leaves + 2 * WIN - 1)

    def leaf_kernel(i, _):
        mine = u_leaf[i]
        live = counts[i]
        for s in range(NBR):
            other = v_ext[place_of(i, s)]
            near = jnp.exp2(mm(mine, other) * LOG2E)
            weights[i * NBR + s] = jnp.where(s < live, near, 0.0).astype(BF16)
        return 0

    lax.fori_loop(0, leaves, leaf_kernel, 0)

    def upward(c):
        cols = pl.ds(starts[c], widths[c])

        def leaf(i, _):
            total = mm(weights[i * NBR], ext[c][place_of(i, 0)])
            for s in range(1, NBR):
                total += mm(weights[i * NBR + s], ext[c][place_of(i, s)])
            mine = ext[c][WIN + i].astype(F32)
            resid = (mine - total * PTS ** (-0.5)).astype(BF16)
            z = mm(inv[i], resid)
            out[pl.ds(pl.multiple_of(i * PTS, PTS), PTS), cols] = z
            up[c][pl.ds(pl.multiple_of(i * SK, SK), SK), :] = mm(
                leaf_pick[i], z.astype(BF16)
            ).astype(BF16)
            return 0

        lax.fori_loop(0, leaves, leaf, 0)

    def gather(c):
        return [
            pltpu.make_async_remote_copy(
                src_ref=top[c],
                dst_ref=gath[c].at[pl.ds(pl.multiple_of(tx * nodes * SK, SK), nodes * SK), :],
                send_sem=top_send.at[c, k - 1],
                recv_sem=top_recv.at[c, k - 1],
                device_id=(lax.rem(tx + k, n_tx), ty),
                device_id_type=MESH,
            )
            for k in range(1, n_tx)
        ]

    def send_top(c):
        for n in range(nodes):
            block = mm(node_pick[n], up[c][pl.ds(n * node_rows, node_rows), :]).astype(BF16)
            top[c][pl.ds(n * SK, SK), :] = block
            gath[c][pl.ds(pl.multiple_of(tx * nodes * SK + n * SK, SK), SK), :] = block
        for copy in gather(c):
            copy.start()

    def downward(c):
        cols = pl.ds(starts[c], widths[c])
        for copy in gather(c):
            copy.wait()
        back = mm(coup_rows[...], gath[c][...])
        for n in range(nodes):
            part = back[n * SK : (n + 1) * SK]
            high = part.astype(BF16)
            low = (part - high.astype(F32)).astype(BF16)
            spread = mm(node_spread[n], high) + mm(node_spread[n], low)
            here = up[c][pl.ds(n * node_rows, node_rows), :].astype(F32)
            down = (here - spread).astype(BF16)
            coup = mm(lone[n], down).astype(BF16)
            for j in range(GROUP):
                i = n * GROUP + j
                rows = pl.ds(i * PTS, PTS)
                out[rows, cols] = out[rows, cols] - mm(
                    inv_cols[i], coup[j * SK : (j + 1) * SK]
                )

    def arrive(c):
        own(c).wait()
        for copy in halo(c):
            copy.wait()

    for c in range(chunks):
        arrive(c)
        upward(c)
        send_top(c)
        if c == 0:
            loads[1].wait()
            loads[2].wait()
        elif c < chunks - 1:
            downward(c - 1)
        if c == chunks - 2:
            downward(c)
    downward(chunks - 1)


def on_device(rhs, pts, leaf_inv, level_one, coupling, neigh, counts, leaf_skel, node_skel):
    rows, cols = rhs.shape
    leaves, nodes = leaf_inv.shape[0], level_one.shape[0]
    n_tx, n_ty = lax.axis_size("tx"), lax.axis_size("ty")
    widths = (128,) * (cols // 128)
    chunks = len(widths)
    side = WIN * PTS
    ext_leaves = leaves + 2 * WIN
    dma = pltpu.SemaphoreType.DMA
    scratch = (
        [pltpu.VMEM((ext_leaves, PTS, w), BF16) for w in widths]
        + [pltpu.VMEM((leaves * SK, w), BF16) for w in widths]
        + [pltpu.VMEM((n_tx * nodes * SK, w), BF16) for w in widths]
        + [pltpu.VMEM((nodes * SK, w), BF16) for w in widths]
        + [
            pltpu.VMEM((leaves * NBR, PTS, PTS), BF16),
            pltpu.VMEM(leaf_inv.shape, BF16),
            pltpu.VMEM(level_one.shape, BF16),
            pltpu.VMEM(coupling.shape[1:], BF16),
            pltpu.VMEM((leaves, PTS, SK), BF16),
            pltpu.VMEM((leaves, SK, PTS), BF16),
            pltpu.VMEM((nodes, SK, GROUP * SK), BF16),
            pltpu.VMEM((nodes, GROUP * SK, SK), BF16),
            pltpu.VMEM((2 * DIM, side // 2), BF16),
            pltpu.VMEM((2 * DIM, side // 2), BF16),
            pltpu.VMEM((2 * DIM, side // 2), BF16),
            pltpu.VMEM((2 * DIM, side // 2), BF16),
            pltpu.VMEM((ext_leaves, 2 * DIM, PTS), BF16),
            pltpu.VMEM((2 * DIM, rows), F32),
            pltpu.VMEM((leaves, PTS, 2 * DIM), BF16),
            dma((chunks, 2)),
            dma((chunks, 2)),
            dma((2,)),
            dma((2,)),
            dma((chunks, n_tx - 1)),
            dma((chunks, n_tx - 1)),
            dma((chunks,)),
            dma((3,)),
        ]
    )
    vmem = pl.BlockSpec(memory_space=pltpu.VMEM)
    smem = pl.BlockSpec(memory_space=pltpu.SMEM)
    hbm = pl.BlockSpec(memory_space=pltpu.HBM)
    return pl.pallas_call(
        functools.partial(device_kernel, (leaves, nodes, widths, n_tx, n_ty)),
        out_shape=pltpu.VMEM((rows, cols), F32),
        in_specs=[hbm, vmem, hbm, hbm, hbm, smem, smem, vmem, vmem],
        out_specs=vmem,
        scratch_shapes=scratch,
        compiler_params=pltpu.CompilerParams(
            collective_id=0, has_side_effects=True, vmem_limit_bytes=50 * 2**20
        ),
        cost_estimate=pl.CostEstimate(
            flops=2 * 6_500_000_000, bytes_accessed=20_000_000, transcendentals=8_400_000
        ),
    )(rhs.reshape(leaves, PTS, cols), pts, leaf_inv, level_one, coupling, neigh.T, counts, leaf_skel, node_skel)


def solution(mesh):
    return jax.shard_map(
        on_device,
        mesh=mesh,
        in_specs=(
            P(("tx", "ty"), None),
            P(None, ("tx", "ty")),
            P(("tx", "ty"), None, None),
            P(("tx", "ty"), None, None),
            P("ty", "tx", None),
            P(("tx", "ty"), None),
            P(("tx", "ty")),
            P(("tx", "ty"), None),
            P(("tx", "ty"), None),
        ),
        out_specs=P(("tx", "ty"), None),
        check_vma=False,
    )
```

```python
import functools
import math

import jax
import jax.numpy as jnp
from jax import lax
from jax.experimental import pallas as pl
from jax.experimental.pallas import tpu as pltpu
from jax.sharding import PartitionSpec as P

PTS = 256
DIM = 8
SK = 128
GROUP = 8
NBR = 8
WIN = 8
WIDE = 256
MESH = pl.DeviceIdType.MESH
F32 = jnp.float32
BF16 = jnp.bfloat16
LOG2E = math.log2(math.e)


def mm(a, b):
    return jnp.dot(a, b, preferred_element_type=F32)


def device_kernel(
    dims,
    rhs,
    pts,
    leaf_inv,
    level_one,
    coupling,
    neigh,
    counts,
    leaf_skel,
    node_skel,
    out,
    *scratch,
):
    leaves, nodes, widths, pieces, n_tx, n_ty = dims
    chunks = len(widths)
    starts = [sum(widths[:c]) for c in range(chunks)]
    groups = [scratch[k * chunks : (k + 1) * chunks] for k in range(5)]
    from_left, from_right, up, gath, top = groups
    scratch = scratch[5 * chunks :]
    (
        mine,
        slot_of,
        weights,
        inv,
        lone,
        coup_rows,
        inv_cols,
        leaf_pick,
        node_pick,
        node_spread,
        p_right,
        p_left,
        p_from_left,
        p_from_right,
        v_ext,
        u_all,
        u_leaf,
        halo_send,
        halo_recv,
        pts_send,
        pts_recv,
        top_send,
        top_recv,
        own_sem,
        load_sem,
    ) = scratch
    tx = lax.axis_index("tx")
    ty = lax.axis_index("ty")
    right = lax.rem(ty + 1, n_ty)
    left = lax.rem(ty + n_ty - 1, n_ty)
    own_rows = leaves * PTS
    side = WIN * PTS
    half = side // 2
    node_rows = GROUP * SK

    barrier = pltpu.get_barrier_semaphore()
    for t in (left, right):
        pl.semaphore_signal(barrier, inc=1, device_id=(tx, t), device_id_type=MESH)
    for k in range(1, n_tx):
        pl.semaphore_signal(
            barrier, inc=1, device_id=(lax.rem(tx + k, n_tx), ty), device_id_type=MESH
        )
    pl.semaphore_wait(barrier, 2 + n_tx - 1)

    def halo(c, p):
        cols = pl.ds(starts[c], widths[c])
        size = WIN // pieces[c]
        far = WIN - (p + 1) * size
        near = p * size
        return (
            pltpu.make_async_remote_copy(
                src_ref=rhs.at[pl.ds(leaves - WIN + far, size), :, cols],
                dst_ref=from_left[c].at[pl.ds(far, size)],
                send_sem=halo_send.at[c, p, 0],
                recv_sem=halo_recv.at[c, p, 0],
                device_id=(tx, right),
                device_id_type=MESH,
            ),
            pltpu.make_async_remote_copy(
                src_ref=rhs.at[pl.ds(near, size), :, cols],
                dst_ref=from_right[c].at[pl.ds(near, size)],
                send_sem=halo_send.at[c, p, 1],
                recv_sem=halo_recv.at[c, p, 1],
                device_id=(tx, left),
                device_id_type=MESH,
            ),
        )

    def points_halo():
        return (
            pltpu.make_async_remote_copy(
                src_ref=p_right,
                dst_ref=p_from_left,
                send_sem=pts_send.at[0],
                recv_sem=pts_recv.at[0],
                device_id=(tx, right),
                device_id_type=MESH,
            ),
            pltpu.make_async_remote_copy(
                src_ref=p_left,
                dst_ref=p_from_right,
                send_sem=pts_send.at[1],
                recv_sem=pts_recv.at[1],
                device_id=(tx, left),
                device_id_type=MESH,
            ),
        )

    def own(h):
        return pltpu.make_async_copy(
            rhs.at[:, :, pl.ds(h * WIDE, WIDE)], mine.at[h, pl.ds(0, leaves)], own_sem.at[h]
        )

    halves = mine.shape[0]

    loads = (
        pltpu.make_async_copy(leaf_inv, inv, load_sem.at[0]),
        pltpu.make_async_copy(coupling.at[0], coup_rows, load_sem.at[1]),
        pltpu.make_async_copy(level_one, lone, load_sem.at[2]),
    )

    coords = pts[...].astype(F32)

    def two_rows(x):
        return jnp.concatenate([x[:, :half], x[:, half:]], axis=0).astype(BF16)

    p_right[...] = two_rows(coords[:, own_rows - side :])
    p_left[...] = two_rows(coords[:, :side])
    for copy in points_halo():
        copy.start()
    for c in range(chunks):
        for p in range(pieces[c]):
            for copy in halo(c, p):
                copy.start()
    for copy in loads:
        copy.start()
    for h in range(halves):
        own(h).start()
        mine[h, leaves] = jnp.zeros((PTS, WIDE), BF16)
    weights[leaves * NBR] = jnp.zeros((PTS, PTS), BF16)

    def tails(x, sign_rows):
        sq = jnp.sum(x * x, axis=0, keepdims=True) * (-0.5 / DIM)
        high = sq.astype(BF16).astype(F32)
        rest = sq - high
        mid = rest.astype(BF16).astype(F32)
        low = rest - mid
        row = lax.broadcasted_iota(jnp.int32, (8, x.shape[1]), 0)
        at = 3 * sign_rows
        parts = jnp.where(
            row == at, high, jnp.where(row == at + 1, mid, jnp.where(row == at + 2, low, 1.0))
        )
        return jnp.where(row < 6, parts, 0.0)

    def put_other(place, x):
        block = jnp.concatenate([x, tails(x, 0)], axis=0).astype(BF16)
        for j in range(x.shape[1] // PTS):
            v_ext[place + j] = block[:, j * PTS : (j + 1) * PTS]

    u_all[...] = jnp.concatenate([coords * (1.0 / DIM), tails(coords, 1)], axis=0)
    put_other(WIN, coords)

    loads[0].wait()

    def leaf_setup(i, _):
        rows = pl.ds(pl.multiple_of(i * PTS, PTS), PTS)
        u_leaf[i] = u_all[:, rows].T.astype(BF16)
        spot = lax.broadcasted_iota(jnp.int32, (PTS, SK), 0)
        spread = (spot == leaf_skel[pl.ds(i, 1), :]).astype(F32)
        leaf_pick[i] = spread.T.astype(BF16)
        inv_cols[i] = mm(inv[i], spread.astype(BF16)).astype(BF16)
        return 0

    lax.fori_loop(0, leaves, leaf_setup, 0)
    for n in range(nodes):
        spot = lax.broadcasted_iota(jnp.int32, (node_rows, SK), 0)
        spread = (spot == node_skel[pl.ds(n, 1), :]).astype(F32)
        node_spread[n] = spread.astype(BF16)
        node_pick[n] = spread.T.astype(BF16)

    for copy in points_halo():
        copy.wait()
    for block, place in ((p_from_left, 0), (p_from_right, WIN + leaves)):
        far = block[...].astype(F32)
        put_other(place, far[:DIM])
        put_other(place + WIN // 2, far[DIM:])

    base = (tx * n_ty + ty) * leaves - WIN

    def place_of(i, s):
        return jnp.clip(neigh[s, i] - base, 0, leaves + 2 * WIN - 1)

    def leaf_kernel(i, _):
        here = u_leaf[i]
        live = counts[i]
        places = [place_of(i, s) for s in range(NBR)]
        first = jnp.where(i < WIN, 0, WIN + leaves)
        for h in range(WIN):
            slot = leaves * NBR
            for s in range(NBR):
                hit = (places[s] == first + h) & (s < live)
                slot = jnp.where(hit, i * NBR + s, slot)
            slot_of[i * WIN + h] = slot
        for s in range(NBR):
            near = jnp.exp2(mm(here, v_ext[places[s]]) * LOG2E)
            weights[i * NBR + s] = jnp.where(s < live, near, 0.0).astype(BF16)
        return 0

    lax.fori_loop(0, leaves, leaf_kernel, 0)

    def rows_of(i, size):
        return pl.ds(pl.multiple_of(i * size, size), size)

    def own_near(h):
        cols = pl.ds(h * WIDE, WIDE)

        def own_place(i, s):
            at = place_of(i, s) - WIN
            return jnp.where((at >= 0) & (at < leaves), at, leaves)

        def leaf(i, _):
            total = mm(weights[i * NBR], mine[h, own_place(i, 0)])
            for s in range(1, NBR):
                total += mm(weights[i * NBR + s], mine[h, own_place(i, s)])
            out[rows_of(i, PTS), cols] = total
            return 0

        lax.fori_loop(0, leaves, leaf, 0, unroll=2)

    def upward(c):
        cols = pl.ds(starts[c], widths[c])
        h, lane = divmod(starts[c], WIDE)

        def with_halo(i, block, places):
            total = out[rows_of(i, PTS), cols]
            for at in places:
                total += mm(weights[slot_of[i * WIN + at]], block[at])
            return total

        for p in range(WIN // 2):
            step = WIN // 2 // pieces[c]
            if p % step == 0:
                for copy in halo(c, p // step):
                    copy.wait()
            low, high = (WIN - 1 - 2 * p, WIN - 2 - 2 * p), (2 * p, 2 * p + 1)

            def leaf(i, _):
                j = leaves - 1 - i
                a = with_halo(i, from_left[c], low)
                b = with_halo(j, from_right[c], high)
                out[rows_of(i, PTS), cols] = a
                out[rows_of(j, PTS), cols] = b
                return 0

            if p < WIN // 2 - 1:
                lax.fori_loop(0, WIN - 2 - 2 * p, leaf, 0)
            done = (WIN - 1 - 2 * p, WIN - 2 - 2 * p, WIN + 2 * p, WIN + 2 * p + 1)
            near = (
                with_halo(done[0], from_left[c], low[:1]),
                with_halo(done[1], from_left[c], low),
                with_halo(done[2], from_right[c], high[:1]),
                with_halo(done[3], from_right[c], high),
            )
            resid = [
                (mine[h, i, :, lane : lane + widths[c]].astype(F32) - t * PTS ** (-0.5)).astype(BF16)
                for i, t in zip(done, near)
            ]
            inner = [mm(inv[i], r) for i, r in zip(done, resid)]
            for i, z in zip(done, inner):
                out[pl.ds(i * PTS, PTS), cols] = z
            for i, z in zip(done, inner):
                up[c][pl.ds(i * SK, SK), :] = mm(leaf_pick[i], z.astype(BF16)).astype(BF16)

    def gather(c):
        return [
            pltpu.make_async_remote_copy(
                src_ref=top[c],
                dst_ref=gath[c].at[pl.ds(pl.multiple_of(tx * nodes * SK, SK), nodes * SK), :],
                send_sem=top_send.at[c, k - 1],
                recv_sem=top_recv.at[c, k - 1],
                device_id=(lax.rem(tx + k, n_tx), ty),
                device_id_type=MESH,
            )
            for k in range(1, n_tx)
        ]

    def send_top(c):
        for n in range(nodes):
            block = mm(node_pick[n], up[c][pl.ds(n * node_rows, node_rows), :]).astype(BF16)
            top[c][pl.ds(n * SK, SK), :] = block
            gath[c][pl.ds(pl.multiple_of(tx * nodes * SK + n * SK, SK), SK), :] = block
        for copy in gather(c):
            copy.start()

    def downward(c):
        cols = pl.ds(starts[c], widths[c])
        for copy in gather(c):
            copy.wait()
        back = mm(coup_rows[...], gath[c][...])
        for n in range(nodes):
            part = back[n * SK : (n + 1) * SK]
            high = part.astype(BF16)
            low = (part - high.astype(F32)).astype(BF16)
            spread = mm(node_spread[n], high) + mm(node_spread[n], low)
            here = up[c][pl.ds(n * node_rows, node_rows), :].astype(F32)
            down = (here - spread).astype(BF16)
            coup = mm(lone[n], down).astype(BF16)
            for j in range(GROUP):
                i = n * GROUP + j
                rows = pl.ds(i * PTS, PTS)
                out[rows, cols] = out[rows, cols] - mm(
                    inv_cols[i], coup[j * SK : (j + 1) * SK]
                )

    for h in range(halves):
        own(h).wait()
    for h in range(halves):
        own_near(h)
    for c in range(chunks):
        upward(c)
        send_top(c)
        if c == 0:
            loads[1].wait()
            loads[2].wait()
        else:
            downward(c - 1)
    downward(chunks - 1)


def on_device(rhs, pts, leaf_inv, level_one, coupling, neigh, counts, leaf_skel, node_skel):
    rows, cols = rhs.shape
    leaves, nodes = leaf_inv.shape[0], level_one.shape[0]
    n_tx, n_ty = lax.axis_size("tx"), lax.axis_size("ty")
    widths = (WIDE,) * (cols // WIDE - 1) + (WIDE // 2,) * 2
    pieces = (1,) * (len(widths) - 1) + (4,)
    chunks = len(widths)
    side = WIN * PTS
    halves = cols // WIDE
    dma = pltpu.SemaphoreType.DMA
    scratch = (
        [pltpu.VMEM((WIN, PTS, w), BF16) for w in widths * 2]
        + [pltpu.VMEM((leaves * SK, w), BF16) for w in widths]
        + [pltpu.VMEM((n_tx * nodes * SK, w), BF16) for w in widths]
        + [pltpu.VMEM((nodes * SK, w), BF16) for w in widths]
        + [
            pltpu.VMEM((halves, leaves + 1, PTS, WIDE), BF16),
            pltpu.SMEM((leaves * WIN,), jnp.int32),
            pltpu.VMEM((leaves * NBR + 1, PTS, PTS), BF16),
            pltpu.VMEM(leaf_inv.shape, BF16),
            pltpu.VMEM(level_one.shape, BF16),
            pltpu.VMEM(coupling.shape[1:], BF16),
            pltpu.VMEM((leaves, PTS, SK), BF16),
            pltpu.VMEM((leaves, SK, PTS), BF16),
            pltpu.VMEM((nodes, SK, GROUP * SK), BF16),
            pltpu.VMEM((nodes, GROUP * SK, SK), BF16),
            pltpu.VMEM((2 * DIM, side // 2), BF16),
            pltpu.VMEM((2 * DIM, side // 2), BF16),
            pltpu.VMEM((2 * DIM, side // 2), BF16),
            pltpu.VMEM((2 * DIM, side // 2), BF16),
            pltpu.VMEM((leaves + 2 * WIN, 2 * DIM, PTS), BF16),
            pltpu.VMEM((2 * DIM, rows), F32),
            pltpu.VMEM((leaves, PTS, 2 * DIM), BF16),
            dma((chunks, max(pieces), 2)),
            dma((chunks, max(pieces), 2)),
            dma((2,)),
            dma((2,)),
            dma((chunks, n_tx - 1)),
            dma((chunks, n_tx - 1)),
            dma((halves,)),
            dma((3,)),
        ]
    )
    vmem = pl.BlockSpec(memory_space=pltpu.VMEM)
    smem = pl.BlockSpec(memory_space=pltpu.SMEM)
    hbm = pl.BlockSpec(memory_space=pltpu.HBM)
    return pl.pallas_call(
        functools.partial(device_kernel, (leaves, nodes, widths, pieces, n_tx, n_ty)),
        out_shape=pltpu.VMEM((rows, cols), F32),
        in_specs=[hbm, vmem, hbm, hbm, hbm, smem, smem, vmem, vmem],
        out_specs=vmem,
        scratch_shapes=scratch,
        compiler_params=pltpu.CompilerParams(
            collective_id=0, has_side_effects=True, vmem_limit_bytes=50 * 2**20
        ),
        cost_estimate=pl.CostEstimate(
            flops=2 * 6_500_000_000, bytes_accessed=20_000_000, transcendentals=8_400_000
        ),
    )(rhs.reshape(leaves, PTS, cols), pts, leaf_inv, level_one, coupling, neigh.T, counts, leaf_skel, node_skel)


def solution(mesh):
    return jax.shard_map(
        on_device,
        mesh=mesh,
        in_specs=(
            P(("tx", "ty"), None),
            P(None, ("tx", "ty")),
            P(("tx", "ty"), None, None),
            P(("tx", "ty"), None, None),
            P("ty", "tx", None),
            P(("tx", "ty"), None),
            P(("tx", "ty")),
            P(("tx", "ty"), None),
            P(("tx", "ty"), None),
        ),
        out_specs=P(("tx", "ty"), None),
        check_vma=False,
    )
```

```python
import functools
import math

import jax
import jax.numpy as jnp
from jax import lax
from jax.experimental import pallas as pl
from jax.experimental.pallas import tpu as pltpu
from jax.sharding import PartitionSpec as P

PTS = 256
DIM = 8
SK = 128
GROUP = 8
NBR = 8
WIN = 8
WIDE = 256
MESH = pl.DeviceIdType.MESH
F32 = jnp.float32
BF16 = jnp.bfloat16
LOG2E = math.log2(math.e)


def mm(a, b):
    return jnp.dot(a, b, preferred_element_type=F32)


def rows_of(i, size):
    return pl.ds(pl.multiple_of(i * size, size), size)


def downward(nodes, coup_rows, gath, up, node_spread, lone, inv_cols, store):
    width = up.shape[1]
    back = mm(coup_rows[...], gath[...])
    for n in range(nodes):
        part = back[n * SK : (n + 1) * SK]
        high = part.astype(BF16)
        low = (part - high.astype(F32)).astype(BF16)
        spread = mm(node_spread[n], jnp.concatenate([high, low], axis=0))
        here = up[pl.ds(n * GROUP * SK, GROUP * SK), :].astype(F32)
        down = (here - spread).astype(BF16)
        coup = mm(lone[n], down).astype(BF16)
        blocks = [coup[j * SK : (j + 1) * SK] for j in range(GROUP)]
        for j in range(0, GROUP, 2):
            i = n * GROUP + j
            cols = inv_cols[i // 2]
            if width <= SK:
                none = jnp.zeros_like(blocks[j])
                pair = jnp.concatenate(
                    [
                        jnp.concatenate([blocks[j], none], axis=1),
                        jnp.concatenate([none, blocks[j + 1]], axis=1),
                    ],
                    axis=0,
                )
                both = mm(cols, pair)
                store(i, both[:, :width])
                store(i + 1, both[:, width:])
            else:
                store(i, mm(cols[:, :SK], blocks[j]))
                store(i + 1, mm(cols[:, SK:], blocks[j + 1]))


def device_kernel(
    dims,
    rhs,
    pts,
    leaf_inv,
    level_one,
    coupling,
    neigh,
    counts,
    leaf_skel,
    node_skel,
    out,
    gath_last,
    up_last,
    coup_rows,
    lone,
    node_spread,
    inv_cols,
    *scratch,
):
    leaves, nodes, widths, pieces, n_tx, n_ty = dims
    chunks = len(widths)
    starts = [sum(widths[:c]) for c in range(chunks)]
    groups = [scratch[k * chunks : (k + 1) * chunks] for k in range(3)]
    from_left, from_right, top = groups
    scratch = scratch[3 * chunks :]
    up = scratch[: chunks - 1] + (up_last,)
    gath = scratch[chunks - 1 : 2 * chunks - 2] + (gath_last,)
    scratch = scratch[2 * chunks - 2 :]
    (
        mine,
        held,
        slot_of,
        weights,
        inv,
        leaf_pick,
        node_pick,
        p_right,
        p_left,
        p_from_left,
        p_from_right,
        v_ext,
        u_all,
        u_leaf,
        halo_send,
        halo_recv,
        pts_send,
        pts_recv,
        top_send,
        top_recv,
        own_sem,
        load_sem,
    ) = scratch
    tx = lax.axis_index("tx")
    ty = lax.axis_index("ty")
    right = lax.rem(ty + 1, n_ty)
    left = lax.rem(ty + n_ty - 1, n_ty)
    own_rows = leaves * PTS
    side = WIN * PTS
    half = side // 2
    node_rows = GROUP * SK

    barrier = pltpu.get_barrier_semaphore()
    for t in (left, right):
        pl.semaphore_signal(barrier, inc=1, device_id=(tx, t), device_id_type=MESH)
    mate = tx + 1 - 2 * lax.rem(tx, 2)
    turns = n_tx // 2
    for t in [mate] + [lax.rem(tx + 2 * k, n_tx) for k in range(1, turns)]:
        pl.semaphore_signal(barrier, inc=1, device_id=(t, ty), device_id_type=MESH)
    pl.semaphore_wait(barrier, 2 + turns)

    def halo(c, p):
        cols = pl.ds(starts[c], widths[c])
        size = WIN // pieces[c]
        far = WIN - (p + 1) * size
        near = p * size
        return (
            pltpu.make_async_remote_copy(
                src_ref=rhs.at[pl.ds(leaves - WIN + far, size), :, cols],
                dst_ref=from_left[c].at[pl.ds(far, size)],
                send_sem=halo_send.at[c, p, 0],
                recv_sem=halo_recv.at[c, p, 0],
                device_id=(tx, right),
                device_id_type=MESH,
            ),
            pltpu.make_async_remote_copy(
                src_ref=rhs.at[pl.ds(near, size), :, cols],
                dst_ref=from_right[c].at[pl.ds(near, size)],
                send_sem=halo_send.at[c, p, 1],
                recv_sem=halo_recv.at[c, p, 1],
                device_id=(tx, left),
                device_id_type=MESH,
            ),
        )

    def points_halo():
        return (
            pltpu.make_async_remote_copy(
                src_ref=p_right,
                dst_ref=p_from_left,
                send_sem=pts_send.at[0],
                recv_sem=pts_recv.at[0],
                device_id=(tx, right),
                device_id_type=MESH,
            ),
            pltpu.make_async_remote_copy(
                src_ref=p_left,
                dst_ref=p_from_right,
                send_sem=pts_send.at[1],
                recv_sem=pts_recv.at[1],
                device_id=(tx, left),
                device_id_type=MESH,
            ),
        )

    def own(h):
        return pltpu.make_async_copy(
            rhs.at[:, :, pl.ds(h * WIDE, WIDE)], mine.at[h, pl.ds(0, leaves)], own_sem.at[h]
        )

    halves = mine.shape[0]

    loads = (
        pltpu.make_async_copy(leaf_inv, inv, load_sem.at[0]),
        pltpu.make_async_copy(coupling.at[0], coup_rows, load_sem.at[1]),
        pltpu.make_async_copy(level_one, lone, load_sem.at[2]),
    )

    coords = pts[...].astype(F32)

    def two_rows(x):
        return jnp.concatenate([x[:, :half], x[:, half:]], axis=0).astype(BF16)

    p_right[...] = two_rows(coords[:, own_rows - side :])
    p_left[...] = two_rows(coords[:, :side])
    for copy in points_halo():
        copy.start()
    for c in range(chunks):
        for p in range(pieces[c]):
            for copy in halo(c, p):
                copy.start()
    for copy in loads:
        copy.start()
    for h in range(halves):
        own(h).start()
        mine[h, leaves] = jnp.zeros((PTS, WIDE), BF16)
    weights[leaves * NBR] = jnp.zeros((PTS, PTS), BF16)

    def tails(x, sign_rows):
        sq = jnp.sum(x * x, axis=0, keepdims=True) * (-0.5 / DIM)
        high = sq.astype(BF16).astype(F32)
        rest = sq - high
        mid = rest.astype(BF16).astype(F32)
        low = rest - mid
        row = lax.broadcasted_iota(jnp.int32, (8, x.shape[1]), 0)
        at = 3 * sign_rows
        parts = jnp.where(
            row == at, high, jnp.where(row == at + 1, mid, jnp.where(row == at + 2, low, 1.0))
        )
        return jnp.where(row < 6, parts, 0.0)

    def put_other(place, x):
        block = jnp.concatenate([x, tails(x, 0)], axis=0).astype(BF16)
        for j in range(x.shape[1] // PTS):
            v_ext[place + j] = block[:, j * PTS : (j + 1) * PTS]

    u_all[...] = jnp.concatenate([coords * (1.0 / DIM), tails(coords, 1)], axis=0)
    put_other(WIN, coords)

    loads[0].wait()

    def leaf_setup(q, _):
        spot = lax.broadcasted_iota(jnp.int32, (PTS, SK), 0)
        for k in range(2):
            i = 2 * q + k
            u_leaf[i] = u_all[:, rows_of(i, PTS)].T.astype(BF16)
            spread = (spot == leaf_skel[pl.ds(i, 1), :]).astype(F32)
            leaf_pick[i] = spread.T.astype(BF16)
            cols = mm(inv[i], spread.astype(BF16)).astype(BF16)
            inv_cols[q, :, k * SK : (k + 1) * SK] = cols
        return 0

    lax.fori_loop(0, leaves // 2, leaf_setup, 0)
    for n in range(nodes):
        spot = lax.broadcasted_iota(jnp.int32, (node_rows, SK), 0)
        spread = (spot == node_skel[pl.ds(n, 1), :]).astype(F32)
        node_spread[n, :, :SK] = spread.astype(BF16)
        node_spread[n, :, SK:] = spread.astype(BF16)
        node_pick[n] = spread.T.astype(BF16)

    for copy in points_halo():
        copy.wait()
    for block, place in ((p_from_left, 0), (p_from_right, WIN + leaves)):
        far = block[...].astype(F32)
        put_other(place, far[:DIM])
        put_other(place + WIN // 2, far[DIM:])

    base = (tx * n_ty + ty) * leaves - WIN

    def place_of(i, s):
        return jnp.clip(neigh[s, i] - base, 0, leaves + 2 * WIN - 1)

    def leaf_kernel(i, _):
        here = u_leaf[i]
        live = counts[i]
        places = [place_of(i, s) for s in range(NBR)]
        first = jnp.where(i < WIN, 0, WIN + leaves)
        for h in range(WIN):
            slot = leaves * NBR
            for s in range(NBR):
                hit = (places[s] == first + h) & (s < live)
                slot = jnp.where(hit, i * NBR + s, slot)
            slot_of[i * WIN + h] = slot
        for s in range(NBR):
            near = jnp.exp2(mm(here, v_ext[places[s]]) * LOG2E)
            weights[i * NBR + s] = jnp.where(s < live, near, 0.0).astype(BF16)
        return 0

    lax.fori_loop(0, leaves, leaf_kernel, 0, unroll=2)

    def own_near(h):
        cols = pl.ds(h * WIDE, WIDE)

        def own_place(i, s):
            at = place_of(i, s) - WIN
            return jnp.where((at >= 0) & (at < leaves), at, leaves)

        def leaf(i, _):
            total = mm(weights[i * NBR], mine[h, own_place(i, 0)])
            for s in range(1, NBR):
                total += mm(weights[i * NBR + s], mine[h, own_place(i, s)])
            out[rows_of(i, PTS), cols] = total
            return 0

        lax.fori_loop(0, leaves, leaf, 0, unroll=4)

    def upward(c):
        cols = pl.ds(starts[c], widths[c])
        h, lane = divmod(starts[c], WIDE)

        def with_halo(i, block, places):
            total = out[rows_of(i, PTS), cols]
            for at in places:
                total += mm(weights[slot_of[i * WIN + at]], block[at])
            return total

        def finish(done, near):
            own_rhs = [mine[h, i, :, lane : lane + widths[c]].astype(F32) for i in done]
            return [(r - t * PTS ** (-0.5)).astype(BF16) for r, t in zip(own_rhs, near)]

        def inverse(done, resid):
            inner = [mm(inv[i], r) for i, r in zip(done, resid)]
            for i, z in zip(done, inner):
                out[rows_of(i, PTS), cols] = z
            for i, z in zip(done, inner):
                up[c][rows_of(i, SK), :] = mm(leaf_pick[i], z.astype(BF16)).astype(BF16)

        for p in range(WIN // 2):
            step = WIN // 2 // pieces[c]
            if p % step == 0:
                for copy in halo(c, p // step):
                    copy.wait()
            if c > 0 and p == (0 if pieces[c] == 1 else WIN // 2 - 2):
                pass_on(c - 1)
            low, high = (WIN - 1 - 2 * p, WIN - 2 - 2 * p), (2 * p, 2 * p + 1)

            def leaf(i, _):
                j = leaves - 1 - i
                a = with_halo(i, from_left[c], low)
                b = with_halo(j, from_right[c], high)
                out[rows_of(i, PTS), cols] = a
                out[rows_of(j, PTS), cols] = b
                return 0

            if p < WIN // 2 - 1:
                lax.fori_loop(0, WIN - 2 - 2 * p, leaf, 0, unroll=2)
            done = (WIN - 1 - 2 * p, WIN - 2 - 2 * p, WIN + 2 * p, WIN + 2 * p + 1)
            near = (
                with_halo(done[0], from_left[c], low[:1]),
                with_halo(done[1], from_left[c], low),
                with_halo(done[2], from_right[c], high[:1]),
                with_halo(done[3], from_right[c], high),
            )
            resid = finish(done, near)
            if pieces[c] > 1:
                inverse(done, resid)
            else:
                for i, r in zip(done, resid):
                    held[i, :, : widths[c]] = r
        if pieces[c] == 1:

            def group(g, _):
                done = [g * 4 + k for k in range(4)]
                inverse(done, [held[i, :, : widths[c]] for i in done])
                return 0

            lax.fori_loop(0, leaves // 4, group, 0)

    def top_copy(c, src, owner, sem, t):
        return pltpu.make_async_remote_copy(
            src_ref=src,
            dst_ref=gath[c].at[rows_of(owner, nodes * SK)],
            send_sem=top_send.at[c, sem],
            recv_sem=top_recv.at[c, sem],
            device_id=(t, ty),
            device_id_type=MESH,
        )

    def far_copies(c):
        return [top_copy(c, top[c], tx, k, lax.rem(tx + 2 * k, n_tx)) for k in range(1, turns)]

    def near_copy(c):
        return top_copy(c, top[c], tx, 0, mate)

    def second_copies(c):
        copies = []
        for k in range(1, turns):
            owner = lax.rem(tx + n_tx - 2 * k, n_tx)
            block = gath[c].at[rows_of(owner, nodes * SK)]
            copies.append(top_copy(c, block, owner, turns - 1 + k, mate))
        return copies

    def send_top(c):
        for n in range(nodes):
            block = mm(node_pick[n], up[c][pl.ds(n * node_rows, node_rows), :]).astype(BF16)
            top[c][pl.ds(n * SK, SK), :] = block
            gath[c][pl.ds(pl.multiple_of(tx * nodes * SK + n * SK, SK), SK), :] = block
        for copy in far_copies(c):
            copy.start()
        near_copy(c).start()

    def pass_on(c):
        for first, second in zip(far_copies(c), second_copies(c)):
            first.wait_recv()
            second.start()

    def gathered(c):
        for copy in far_copies(c):
            copy.wait_send()
        near_copy(c).wait()
        for copy in second_copies(c):
            copy.wait()

    def correct(c):
        cols = pl.ds(starts[c], widths[c])

        def store(i, x):
            rows = pl.ds(i * PTS, PTS)
            out[rows, cols] = out[rows, cols] - x

        gathered(c)
        downward(nodes, coup_rows, gath[c], up[c], node_spread, lone, inv_cols, store)

    for h in range(halves):
        own(h).wait()
    for h in range(halves):
        own_near(h)
    last = chunks - 1
    for c in range(chunks):
        upward(c)
        send_top(c)
        if c == 0:
            loads[1].wait()
            loads[2].wait()
        else:
            correct(c - 1)
    pass_on(last)
    gathered(last)


def last_kernel(nodes, start, held, gath, up, coup_rows, lone, node_spread, inv_cols, out, sol, sem):
    ready = pltpu.make_async_copy(
        held.at[:, pl.ds(0, start)], out.at[:, pl.ds(0, start)], sem.at[nodes]
    )
    ready.start()
    width = held.shape[1] - start
    part = held.shape[0] // nodes

    def done(n):
        rows = pl.ds(n * part, part)
        return pltpu.make_async_copy(sol.at[rows], out.at[rows, pl.ds(start, width)], sem.at[n])

    def store(i, x):
        rows = pl.ds(i * PTS, PTS)
        sol[rows, :] = held[rows, pl.ds(start, width)] - x
        if (i + 1) % GROUP == 0:
            done(i // GROUP).start()

    downward(nodes, coup_rows, gath, up, node_spread, lone, inv_cols, store)
    ready.wait()
    for n in range(nodes):
        done(n).wait()


def on_device(rhs, pts, leaf_inv, level_one, coupling, neigh, counts, leaf_skel, node_skel):
    rows, cols = rhs.shape
    leaves, nodes = leaf_inv.shape[0], level_one.shape[0]
    n_tx, n_ty = lax.axis_size("tx"), lax.axis_size("ty")
    widths = (WIDE,) * (cols // WIDE - 1) + (WIDE // 2,) * 2
    pieces = (1,) * (len(widths) - 1) + (4,)
    chunks = len(widths)
    side = WIN * PTS
    halves = cols // WIDE
    dma = pltpu.SemaphoreType.DMA
    tops = n_tx * nodes * SK
    scratch = (
        [pltpu.VMEM((WIN, PTS, w), BF16) for w in widths * 2]
        + [pltpu.VMEM((nodes * SK, w), BF16) for w in widths]
        + [pltpu.VMEM((leaves * SK, w), BF16) for w in widths[:-1]]
        + [pltpu.VMEM((tops, w), BF16) for w in widths[:-1]]
        + [
            pltpu.VMEM((halves, leaves + 1, PTS, WIDE), BF16),
            pltpu.VMEM((leaves, PTS, WIDE), BF16),
            pltpu.SMEM((leaves * WIN,), jnp.int32),
            pltpu.VMEM((leaves * NBR + 1, PTS, PTS), BF16),
            pltpu.VMEM(leaf_inv.shape, BF16),
            pltpu.VMEM((leaves, SK, PTS), BF16),
            pltpu.VMEM((nodes, SK, GROUP * SK), BF16),
            pltpu.VMEM((2 * DIM, side // 2), BF16),
            pltpu.VMEM((2 * DIM, side // 2), BF16),
            pltpu.VMEM((2 * DIM, side // 2), BF16),
            pltpu.VMEM((2 * DIM, side // 2), BF16),
            pltpu.VMEM((leaves + 2 * WIN, 2 * DIM, PTS), BF16),
            pltpu.VMEM((2 * DIM, rows), F32),
            pltpu.VMEM((leaves, PTS, 2 * DIM), BF16),
            dma((chunks, max(pieces), 2)),
            dma((chunks, max(pieces), 2)),
            dma((2,)),
            dma((2,)),
            dma((chunks, n_tx - 1)),
            dma((chunks, n_tx - 1)),
            dma((halves,)),
            dma((3,)),
        ]
    )
    vmem = pl.BlockSpec(memory_space=pltpu.VMEM)
    smem = pl.BlockSpec(memory_space=pltpu.SMEM)
    hbm = pl.BlockSpec(memory_space=pltpu.HBM)
    kept = (
        pltpu.VMEM((rows, cols), F32),
        pltpu.VMEM((tops, widths[-1]), BF16),
        pltpu.VMEM((leaves * SK, widths[-1]), BF16),
        pltpu.VMEM(coupling.shape[1:], BF16),
        pltpu.VMEM(level_one.shape, BF16),
        pltpu.VMEM((nodes, GROUP * SK, 2 * SK), BF16),
        pltpu.VMEM((leaves // 2, PTS, 2 * SK), BF16),
    )
    parts = pl.pallas_call(
        functools.partial(device_kernel, (leaves, nodes, widths, pieces, n_tx, n_ty)),
        out_shape=kept,
        in_specs=[hbm, vmem, hbm, hbm, hbm, smem, smem, vmem, vmem],
        out_specs=(vmem,) * len(kept),
        scratch_shapes=scratch,
        compiler_params=pltpu.CompilerParams(
            collective_id=0, has_side_effects=True, vmem_limit_bytes=42 * 2**20
        ),
        cost_estimate=pl.CostEstimate(
            flops=2 * 6_500_000_000, bytes_accessed=20_000_000, transcendentals=8_400_000
        ),
    )(
        rhs.reshape(leaves, PTS, cols),
        pts,
        leaf_inv,
        level_one,
        coupling,
        neigh.T,
        counts,
        leaf_skel,
        node_skel,
    )
    return pl.pallas_call(
        functools.partial(last_kernel, nodes, cols - widths[-1]),
        out_shape=jax.ShapeDtypeStruct((rows, cols), F32),
        in_specs=[vmem] * len(kept),
        out_specs=hbm,
        scratch_shapes=[pltpu.VMEM((rows, widths[-1]), F32), dma((nodes + 1,))],
        compiler_params=pltpu.CompilerParams(vmem_limit_bytes=16 * 2**20),
        cost_estimate=pl.CostEstimate(
            flops=2 * 250_000_000, bytes_accessed=8_400_000, transcendentals=0
        ),
    )(*parts)


def solution(mesh):
    return jax.shard_map(
        on_device,
        mesh=mesh,
        in_specs=(
            P(("tx", "ty"), None),
            P(None, ("tx", "ty")),
            P(("tx", "ty"), None, None),
            P(("tx", "ty"), None, None),
            P("ty", "tx", None),
            P(("tx", "ty"), None),
            P(("tx", "ty")),
            P(("tx", "ty"), None),
            P(("tx", "ty"), None),
        ),
        out_specs=P(("tx", "ty"), None),
        check_vma=False,
    )
```

```python
import functools
import math

import jax
import jax.numpy as jnp
from jax import lax
from jax.experimental import pallas as pl
from jax.experimental.pallas import tpu as pltpu
from jax.sharding import PartitionSpec as P

PTS = 256
DIM = 8
SK = 128
GROUP = 8
NBR = 8
WIN = 8
WIDE = 256
MESH = pl.DeviceIdType.MESH
F32 = jnp.float32
BF16 = jnp.bfloat16
LOG2E = math.log2(math.e)


def mm(a, b):
    return jnp.dot(a, b, preferred_element_type=F32)


def rows_of(i, size):
    return pl.ds(pl.multiple_of(i * size, size), size)


def downward(which, coup_rows, gath, up, node_spread, lone, inv_cols, store):
    width = up.shape[1]
    first = which[0]
    back = mm(coup_rows[first * SK : (which[-1] + 1) * SK, :], gath[...])
    for n in which:
        part = back[(n - first) * SK : (n - first + 1) * SK]
        high = part.astype(BF16)
        low = (part - high.astype(F32)).astype(BF16)
        spread = mm(node_spread[n], jnp.concatenate([high, low], axis=0))
        here = up[pl.ds(n * GROUP * SK, GROUP * SK), :].astype(F32)
        down = (here - spread).astype(BF16)
        coup = mm(lone[n], down).astype(BF16)
        blocks = [coup[j * SK : (j + 1) * SK] for j in range(GROUP)]
        for j in range(0, GROUP, 2):
            i = n * GROUP + j
            cols = inv_cols[i // 2]
            if width <= SK:
                none = jnp.zeros_like(blocks[j])
                pair = jnp.concatenate(
                    [
                        jnp.concatenate([blocks[j], none], axis=1),
                        jnp.concatenate([none, blocks[j + 1]], axis=1),
                    ],
                    axis=0,
                )
                both = mm(cols, pair)
                store(i, both[:, :width])
                store(i + 1, both[:, width:])
            else:
                store(i, mm(cols[:, :SK], blocks[j]))
                store(i + 1, mm(cols[:, SK:], blocks[j + 1]))


def device_kernel(
    dims,
    rhs,
    pts,
    leaf_inv,
    level_one,
    coupling,
    neigh,
    counts,
    leaf_skel,
    node_skel,
    out,
    gath_last,
    up_last,
    coup_rows,
    lone,
    node_spread,
    inv_cols,
    *scratch,
):
    leaves, nodes, widths, pieces, n_tx, n_ty = dims
    chunks = len(widths)
    starts = [sum(widths[:c]) for c in range(chunks)]
    groups = [scratch[k * chunks : (k + 1) * chunks] for k in range(3)]
    from_left, from_right, top = groups
    scratch = scratch[3 * chunks :]
    up = scratch[: chunks - 1] + (up_last,)
    gath = scratch[chunks - 1 : 2 * chunks - 2] + (gath_last,)
    scratch = scratch[2 * chunks - 2 :]
    (
        mine,
        held,
        slot_of,
        weights,
        inv,
        leaf_pick,
        node_pick,
        p_right,
        p_left,
        p_from_left,
        p_from_right,
        v_ext,
        u_all,
        u_leaf,
        halo_send,
        halo_recv,
        pts_send,
        pts_recv,
        top_send,
        top_recv,
        own_sem,
        load_sem,
    ) = scratch
    tx = lax.axis_index("tx")
    ty = lax.axis_index("ty")
    right = lax.rem(ty + 1, n_ty)
    left = lax.rem(ty + n_ty - 1, n_ty)
    own_rows = leaves * PTS
    side = WIN * PTS
    half = side // 2
    node_rows = GROUP * SK

    barrier = pltpu.get_barrier_semaphore()
    for t in (left, right):
        pl.semaphore_signal(barrier, inc=1, device_id=(tx, t), device_id_type=MESH)
    mate = tx + 1 - 2 * lax.rem(tx, 2)
    turns = n_tx // 2
    hops = (*(k for k in range(1, turns) if 2 * k != turns), turns // 2)
    for t in [mate] + [lax.rem(tx + 2 * k, n_tx) for k in range(1, turns)]:
        pl.semaphore_signal(barrier, inc=1, device_id=(t, ty), device_id_type=MESH)
    pl.semaphore_wait(barrier, 2 + turns)

    def halo(c, p):
        cols = pl.ds(starts[c], widths[c])
        size = WIN // pieces[c]
        far = WIN - (p + 1) * size
        near = p * size
        return (
            pltpu.make_async_remote_copy(
                src_ref=rhs.at[pl.ds(leaves - WIN + far, size), :, cols],
                dst_ref=from_left[c].at[pl.ds(far, size)],
                send_sem=halo_send.at[c, p, 0],
                recv_sem=halo_recv.at[c, p, 0],
                device_id=(tx, right),
                device_id_type=MESH,
            ),
            pltpu.make_async_remote_copy(
                src_ref=rhs.at[pl.ds(near, size), :, cols],
                dst_ref=from_right[c].at[pl.ds(near, size)],
                send_sem=halo_send.at[c, p, 1],
                recv_sem=halo_recv.at[c, p, 1],
                device_id=(tx, left),
                device_id_type=MESH,
            ),
        )

    def points_halo():
        return (
            pltpu.make_async_remote_copy(
                src_ref=p_right,
                dst_ref=p_from_left,
                send_sem=pts_send.at[0],
                recv_sem=pts_recv.at[0],
                device_id=(tx, right),
                device_id_type=MESH,
            ),
            pltpu.make_async_remote_copy(
                src_ref=p_left,
                dst_ref=p_from_right,
                send_sem=pts_send.at[1],
                recv_sem=pts_recv.at[1],
                device_id=(tx, left),
                device_id_type=MESH,
            ),
        )

    def own(h):
        return pltpu.make_async_copy(
            rhs.at[:, :, pl.ds(h * WIDE, WIDE)], mine.at[h, pl.ds(0, leaves)], own_sem.at[h]
        )

    halves = mine.shape[0]

    loads = (
        pltpu.make_async_copy(leaf_inv, inv, load_sem.at[0]),
        pltpu.make_async_copy(coupling.at[0], coup_rows, load_sem.at[1]),
        pltpu.make_async_copy(level_one, lone, load_sem.at[2]),
    )

    for copy in halo(0, 0):
        copy.start()
    coords = pts[...].astype(F32)

    def two_rows(x):
        return jnp.concatenate([x[:, :half], x[:, half:]], axis=0).astype(BF16)

    p_right[...] = two_rows(coords[:, own_rows - side :])
    p_left[...] = two_rows(coords[:, :side])
    for copy in points_halo():
        copy.start()
    for c in range(chunks):
        for p in range(0 if c else 1, pieces[c]):
            for copy in halo(c, p):
                copy.start()
    for copy in loads:
        copy.start()
    for h in range(halves):
        own(h).start()
        mine[h, leaves] = jnp.zeros((PTS, WIDE), BF16)
    weights[leaves * NBR] = jnp.zeros((PTS, PTS), BF16)

    def tails(x, sign_rows):
        sq = jnp.sum(x * x, axis=0, keepdims=True) * (-0.5 / DIM)
        high = sq.astype(BF16).astype(F32)
        rest = sq - high
        mid = rest.astype(BF16).astype(F32)
        low = rest - mid
        row = lax.broadcasted_iota(jnp.int32, (8, x.shape[1]), 0)
        at = 3 * sign_rows
        parts = jnp.where(
            row == at, high, jnp.where(row == at + 1, mid, jnp.where(row == at + 2, low, 1.0))
        )
        return jnp.where(row < 6, parts, 0.0)

    def put_other(place, x):
        block = jnp.concatenate([x, tails(x, 0)], axis=0).astype(BF16)
        for j in range(x.shape[1] // PTS):
            v_ext[place + j] = block[:, j * PTS : (j + 1) * PTS]

    u_all[...] = jnp.concatenate([coords * (1.0 / DIM), tails(coords, 1)], axis=0)
    put_other(WIN, coords)

    loads[0].wait()

    def leaf_setup(q, _):
        spot = lax.broadcasted_iota(jnp.int32, (PTS, SK), 0)
        for k in range(2):
            i = 2 * q + k
            u_leaf[i] = u_all[:, rows_of(i, PTS)].T.astype(BF16)
            spread = (spot == leaf_skel[pl.ds(i, 1), :]).astype(F32)
            leaf_pick[i] = spread.T.astype(BF16)
            cols = mm(inv[i], spread.astype(BF16)).astype(BF16)
            inv_cols[q, :, k * SK : (k + 1) * SK] = cols
        return 0

    lax.fori_loop(0, leaves // 2, leaf_setup, 0)
    for n in range(nodes):
        spot = lax.broadcasted_iota(jnp.int32, (node_rows, SK), 0)
        spread = (spot == node_skel[pl.ds(n, 1), :]).astype(F32)
        node_spread[n, :, :SK] = spread.astype(BF16)
        node_spread[n, :, SK:] = spread.astype(BF16)
        node_pick[n] = spread.T.astype(BF16)

    for copy in points_halo():
        copy.wait()
    for block, place in ((p_from_left, 0), (p_from_right, WIN + leaves)):
        far = block[...].astype(F32)
        put_other(place, far[:DIM])
        put_other(place + WIN // 2, far[DIM:])

    base = (tx * n_ty + ty) * leaves - WIN

    def place_of(i, s):
        return jnp.clip(neigh[s, i] - base, 0, leaves + 2 * WIN - 1)

    def leaf_kernel(i, _):
        here = u_leaf[i]
        live = counts[i]
        places = [place_of(i, s) for s in range(NBR)]
        first = jnp.where(i < WIN, 0, WIN + leaves)
        for h in range(WIN):
            slot = leaves * NBR
            for s in range(NBR):
                hit = (places[s] == first + h) & (s < live)
                slot = jnp.where(hit, i * NBR + s, slot)
            slot_of[i * WIN + h] = slot
        for s in range(NBR):
            near = jnp.exp2(mm(here, v_ext[places[s]]) * LOG2E)
            weights[i * NBR + s] = jnp.where(s < live, near, 0.0).astype(BF16)
        return 0

    lax.fori_loop(0, leaves, leaf_kernel, 0, unroll=2)

    def own_near(h):
        cols = pl.ds(h * WIDE, WIDE)

        def own_place(i, s):
            at = place_of(i, s) - WIN
            return jnp.where((at >= 0) & (at < leaves), at, leaves)

        def leaf(i, _):
            total = mm(weights[i * NBR], mine[h, own_place(i, 0)])
            for s in range(1, NBR):
                total += mm(weights[i * NBR + s], mine[h, own_place(i, s)])
            out[rows_of(i, PTS), cols] = total
            return 0

        lax.fori_loop(0, leaves, leaf, 0, unroll=8)

    def upward(c):
        cols = pl.ds(starts[c], widths[c])
        h, lane = divmod(starts[c], WIDE)

        def with_halo(i, block, places):
            total = out[rows_of(i, PTS), cols]
            for at in places:
                total += mm(weights[slot_of[i * WIN + at]], block[at])
            return total

        def finish(done, near):
            own_rhs = [mine[h, i, :, lane : lane + widths[c]].astype(F32) for i in done]
            return [(r - t * PTS ** (-0.5)).astype(BF16) for r, t in zip(own_rhs, near)]

        def inverse(done, resid):
            inner = [mm(inv[i], r) for i, r in zip(done, resid)]
            for i, z in zip(done, inner):
                out[rows_of(i, PTS), cols] = z
            for i, z in zip(done, inner):
                up[c][rows_of(i, SK), :] = mm(leaf_pick[i], z.astype(BF16)).astype(BF16)

        for p in range(WIN // 2):
            if c > 0 and p == (0 if c < chunks - 1 else WIN // 2 - 2):
                pass_on(c - 1, hops)
            step = WIN // 2 // pieces[c]
            if p % step == 0:
                for copy in halo(c, p // step):
                    copy.wait()
            low, high = (WIN - 1 - 2 * p, WIN - 2 - 2 * p), (2 * p, 2 * p + 1)

            def leaf(i, _):
                j = leaves - 1 - i
                a = with_halo(i, from_left[c], low)
                b = with_halo(j, from_right[c], high)
                out[rows_of(i, PTS), cols] = a
                out[rows_of(j, PTS), cols] = b
                return 0

            if p < WIN // 2 - 1:
                lax.fori_loop(0, WIN - 2 - 2 * p, leaf, 0, unroll=2)
            done = (WIN - 1 - 2 * p, WIN - 2 - 2 * p, WIN + 2 * p, WIN + 2 * p + 1)
            near = (
                with_halo(done[0], from_left[c], low[:1]),
                with_halo(done[1], from_left[c], low),
                with_halo(done[2], from_right[c], high[:1]),
                with_halo(done[3], from_right[c], high),
            )
            resid = finish(done, near)
            if c == chunks - 1:
                inverse(done, resid)
            else:
                for i, r in zip(done, resid):
                    held[i, :, : widths[c]] = r
        if c < chunks - 1:

            def group(g, _):
                done = [g * 4 + k for k in range(4)]
                inverse(done, [held[i, :, : widths[c]] for i in done])
                return 0

            lax.fori_loop(0, leaves // 4, group, 0, unroll=2)

    def top_copy(c, src, owner, sem, t):
        return pltpu.make_async_remote_copy(
            src_ref=src,
            dst_ref=gath[c].at[rows_of(owner, nodes * SK)],
            send_sem=top_send.at[c, sem],
            recv_sem=top_recv.at[c, sem],
            device_id=(t, ty),
            device_id_type=MESH,
        )

    def far_copy(c, k):
        return top_copy(c, top[c], tx, k, lax.rem(tx + 2 * k, n_tx))

    def near_copy(c):
        return top_copy(c, top[c], tx, 0, mate)

    def second_copy(c, k):
        owner = lax.rem(tx + n_tx - 2 * k, n_tx)
        block = gath[c].at[rows_of(owner, nodes * SK)]
        return top_copy(c, block, owner, turns - 1 + k, mate)

    def send_top(c):
        for n in range(nodes):
            block = mm(node_pick[n], up[c][pl.ds(n * node_rows, node_rows), :]).astype(BF16)
            top[c][pl.ds(n * SK, SK), :] = block
            gath[c][pl.ds(pl.multiple_of(tx * nodes * SK + n * SK, SK), SK), :] = block
        for k in hops:
            far_copy(c, k).start()
        near_copy(c).start()

    def pass_on(c, which):
        for k in which:
            far_copy(c, k).wait_recv()
            second_copy(c, k).start()

    def gathered(c):
        for k in hops:
            far_copy(c, k).wait_send()
        near_copy(c).wait()
        for k in hops:
            second_copy(c, k).wait()

    def correct(c, which):
        cols = pl.ds(starts[c], widths[c])

        def store(i, x):
            rows = pl.ds(i * PTS, PTS)
            out[rows, cols] = out[rows, cols] - x

        downward(which, coup_rows, gath[c], up[c], node_spread, lone, inv_cols, store)

    for h in range(halves):
        own(h).wait()
    for h in range(halves):
        own_near(h)
    last = chunks - 1
    for c in range(chunks):
        upward(c)
        send_top(c)
    loads[1].wait()
    loads[2].wait()
    for c in range(last):
        gathered(c)
    for c in range(last - 1):
        correct(c, range(nodes))
    pass_on(last, hops[:-1])
    for n in range(nodes):
        if n == nodes - 1:
            pass_on(last, hops[-1:])
        correct(last - 1, range(n, n + 1))
    gathered(last)


def last_kernel(nodes, start, held, gath, up, coup_rows, lone, node_spread, inv_cols, out, sol, sem):
    width = held.shape[1] - start
    part = held.shape[0] // (2 * nodes)

    def ready(b):
        here = (pl.ds(b * part, part), pl.ds(0, start))
        return pltpu.make_async_copy(held.at[here], out.at[here], sem.at[0, b])

    def done(b):
        rows = pl.ds(b * part, part)
        return pltpu.make_async_copy(sol.at[rows], out.at[rows, pl.ds(start, width)], sem.at[1, b])

    def store(i, x):
        rows = pl.ds(i * PTS, PTS)
        sol[rows, :] = held[rows, pl.ds(start, width)] - x
        if (i + 1) % (GROUP // 2) == 0:
            done(i // (GROUP // 2)).start()

    for b in range(2 * nodes):
        ready(b).start()
    downward(range(nodes), coup_rows, gath, up, node_spread, lone, inv_cols, store)
    for b in range(2 * nodes):
        ready(b).wait()
        done(b).wait()


def on_device(rhs, pts, leaf_inv, level_one, coupling, neigh, counts, leaf_skel, node_skel):
    rows, cols = rhs.shape
    leaves, nodes = leaf_inv.shape[0], level_one.shape[0]
    n_tx, n_ty = lax.axis_size("tx"), lax.axis_size("ty")
    widths = (WIDE,) * (cols // WIDE - 1) + (WIDE // 2,) * 2
    pieces = (4,) + (1,) * (len(widths) - 2) + (4,)
    chunks = len(widths)
    side = WIN * PTS
    halves = cols // WIDE
    dma = pltpu.SemaphoreType.DMA
    tops = n_tx * nodes * SK
    scratch = (
        [pltpu.VMEM((WIN, PTS, w), BF16) for w in widths * 2]
        + [pltpu.VMEM((nodes * SK, w), BF16) for w in widths]
        + [pltpu.VMEM((leaves * SK, w), BF16) for w in widths[:-1]]
        + [pltpu.VMEM((tops, w), BF16) for w in widths[:-1]]
        + [
            pltpu.VMEM((halves, leaves + 1, PTS, WIDE), BF16),
            pltpu.VMEM((leaves, PTS, WIDE), BF16),
            pltpu.SMEM((leaves * WIN,), jnp.int32),
            pltpu.VMEM((leaves * NBR + 1, PTS, PTS), BF16),
            pltpu.VMEM(leaf_inv.shape, BF16),
            pltpu.VMEM((leaves, SK, PTS), BF16),
            pltpu.VMEM((nodes, SK, GROUP * SK), BF16),
            pltpu.VMEM((2 * DIM, side // 2), BF16),
            pltpu.VMEM((2 * DIM, side // 2), BF16),
            pltpu.VMEM((2 * DIM, side // 2), BF16),
            pltpu.VMEM((2 * DIM, side // 2), BF16),
            pltpu.VMEM((leaves + 2 * WIN, 2 * DIM, PTS), BF16),
            pltpu.VMEM((2 * DIM, rows), F32),
            pltpu.VMEM((leaves, PTS, 2 * DIM), BF16),
            dma((chunks, max(pieces), 2)),
            dma((chunks, max(pieces), 2)),
            dma((2,)),
            dma((2,)),
            dma((chunks, n_tx - 1)),
            dma((chunks, n_tx - 1)),
            dma((halves,)),
            dma((3,)),
        ]
    )
    vmem = pl.BlockSpec(memory_space=pltpu.VMEM)
    smem = pl.BlockSpec(memory_space=pltpu.SMEM)
    hbm = pl.BlockSpec(memory_space=pltpu.HBM)
    kept = (
        pltpu.VMEM((rows, cols), F32),
        pltpu.VMEM((tops, widths[-1]), BF16),
        pltpu.VMEM((leaves * SK, widths[-1]), BF16),
        pltpu.VMEM(coupling.shape[1:], BF16),
        pltpu.VMEM(level_one.shape, BF16),
        pltpu.VMEM((nodes, GROUP * SK, 2 * SK), BF16),
        pltpu.VMEM((leaves // 2, PTS, 2 * SK), BF16),
    )
    parts = pl.pallas_call(
        functools.partial(device_kernel, (leaves, nodes, widths, pieces, n_tx, n_ty)),
        out_shape=kept,
        in_specs=[hbm, vmem, hbm, hbm, hbm, smem, smem, vmem, vmem],
        out_specs=(vmem,) * len(kept),
        scratch_shapes=scratch,
        compiler_params=pltpu.CompilerParams(
            collective_id=0, has_side_effects=True, vmem_limit_bytes=42 * 2**20
        ),
        cost_estimate=pl.CostEstimate(
            flops=2 * 6_500_000_000, bytes_accessed=20_000_000, transcendentals=8_400_000
        ),
    )(
        rhs.reshape(leaves, PTS, cols),
        pts,
        leaf_inv,
        level_one,
        coupling,
        neigh.T,
        counts,
        leaf_skel,
        node_skel,
    )
    return pl.pallas_call(
        functools.partial(last_kernel, nodes, cols - widths[-1]),
        out_shape=jax.ShapeDtypeStruct((rows, cols), F32),
        in_specs=[vmem] * len(kept),
        out_specs=hbm,
        scratch_shapes=[
            pltpu.VMEM((rows, widths[-1]), F32),
            dma((2, 2 * nodes)),
        ],
        compiler_params=pltpu.CompilerParams(vmem_limit_bytes=16 * 2**20),
        cost_estimate=pl.CostEstimate(
            flops=2 * 250_000_000, bytes_accessed=8_400_000, transcendentals=0
        ),
    )(*parts)


def solution(mesh):
    return jax.shard_map(
        on_device,
        mesh=mesh,
        in_specs=(
            P(("tx", "ty"), None),
            P(None, ("tx", "ty")),
            P(("tx", "ty"), None, None),
            P(("tx", "ty"), None, None),
            P("ty", "tx", None),
            P(("tx", "ty"), None),
            P(("tx", "ty")),
            P(("tx", "ty"), None),
            P(("tx", "ty"), None),
        ),
        out_specs=P(("tx", "ty"), None),
        check_vma=False,
    )
```

```python
import functools
import math

import jax
import jax.numpy as jnp
from jax import lax
from jax.experimental import pallas as pl
from jax.experimental.pallas import tpu as pltpu
from jax.sharding import PartitionSpec as P

PTS = 256
DIM = 8
SK = 128
GROUP = 8
NBR = 8
WIN = 8
WIDE = 256
MESH = pl.DeviceIdType.MESH
F32 = jnp.float32
BF16 = jnp.bfloat16
LOG2E = math.log2(math.e)


def mm(a, b):
    return jnp.dot(a, b, preferred_element_type=F32)


def rows_of(i, size):
    return pl.ds(pl.multiple_of(i * size, size), size)


def downward(which, coup_rows, gath, up, node_spread, lone, inv_cols, store):
    width = up.shape[1]
    first = which[0]
    back = mm(coup_rows[first * SK : (which[-1] + 1) * SK, :], gath[...])
    for n in which:
        part = back[(n - first) * SK : (n - first + 1) * SK]
        high = part.astype(BF16)
        low = (part - high.astype(F32)).astype(BF16)
        spread = mm(node_spread[n], jnp.concatenate([high, low], axis=0))
        here = up[pl.ds(n * GROUP * SK, GROUP * SK), :].astype(F32)
        down = (here - spread).astype(BF16)
        coup = mm(lone[n], down).astype(BF16)
        blocks = [coup[j * SK : (j + 1) * SK] for j in range(GROUP)]
        for j in range(0, GROUP, 2):
            i = n * GROUP + j
            cols = inv_cols[i // 2]
            if width <= SK:
                none = jnp.zeros_like(blocks[j])
                pair = jnp.concatenate(
                    [
                        jnp.concatenate([blocks[j], none], axis=1),
                        jnp.concatenate([none, blocks[j + 1]], axis=1),
                    ],
                    axis=0,
                )
                both = mm(cols, pair)
                store(i, both[:, :width])
                store(i + 1, both[:, width:])
            else:
                store(i, mm(cols[:, :SK], blocks[j]))
                store(i + 1, mm(cols[:, SK:], blocks[j + 1]))


def device_kernel(
    dims,
    rhs,
    pts_in,
    leaf_inv,
    level_one,
    coupling,
    neigh_in,
    counts_in,
    leaf_skel_in,
    node_skel_in,
    out,
    gath_last,
    up_last,
    coup_rows,
    lone,
    node_spread,
    inv_cols,
    *scratch,
):
    leaves, nodes, widths, pieces, n_tx, n_ty = dims
    chunks = len(widths)
    starts = [sum(widths[:c]) for c in range(chunks)]
    groups = [scratch[k * chunks : (k + 1) * chunks] for k in range(3)]
    from_left, from_right, top = groups
    scratch = scratch[3 * chunks :]
    up = scratch[: chunks - 1] + (up_last,)
    gath = scratch[chunks - 1 : 2 * chunks - 2] + (gath_last,)
    scratch = scratch[2 * chunks - 2 :]
    (
        mine,
        held,
        slot_of,
        weights,
        inv,
        leaf_pick,
        node_pick,
        p_right,
        p_left,
        p_from_left,
        p_from_right,
        v_ext,
        u_all,
        u_leaf,
        halo_send,
        halo_recv,
        pts_send,
        pts_recv,
        top_send,
        top_recv,
        own_sem,
        load_sem,
        pts,
        leaf_skel,
        node_skel,
        neigh,
        counts,
        small_sem,
    ) = scratch
    tx = lax.axis_index("tx")
    ty = lax.axis_index("ty")
    right = lax.rem(ty + 1, n_ty)
    left = lax.rem(ty + n_ty - 1, n_ty)
    own_rows = leaves * PTS
    side = WIN * PTS
    half = side // 2
    node_rows = GROUP * SK

    barrier = pltpu.get_barrier_semaphore()
    for t in (left, right):
        pl.semaphore_signal(barrier, inc=1, device_id=(tx, t), device_id_type=MESH)
    mate = tx + 1 - 2 * lax.rem(tx, 2)
    turns = n_tx // 2
    hops = (*(k for k in range(1, turns) if 2 * k != turns), turns // 2)
    for t in [mate] + [lax.rem(tx + 2 * k, n_tx) for k in range(1, turns)]:
        pl.semaphore_signal(barrier, inc=1, device_id=(t, ty), device_id_type=MESH)
    pl.semaphore_wait(barrier, 2 + turns)

    small = [
        pltpu.make_async_copy(a, b, small_sem.at[k])
        for k, (a, b) in enumerate(
            ((pts_in, pts), (leaf_skel_in, leaf_skel), (node_skel_in, node_skel), (neigh_in, neigh), (counts_in, counts),)
        )
    ]
    for copy in small:
        copy.start()

    def halo(c, p):
        cols = pl.ds(starts[c], widths[c])
        size = WIN // pieces[c]
        far = WIN - (p + 1) * size
        near = p * size
        return (
            pltpu.make_async_remote_copy(
                src_ref=rhs.at[pl.ds(leaves - WIN + far, size), :, cols],
                dst_ref=from_left[c].at[pl.ds(far, size)],
                send_sem=halo_send.at[c, p, 0],
                recv_sem=halo_recv.at[c, p, 0],
                device_id=(tx, right),
                device_id_type=MESH,
            ),
            pltpu.make_async_remote_copy(
                src_ref=rhs.at[pl.ds(near, size), :, cols],
                dst_ref=from_right[c].at[pl.ds(near, size)],
                send_sem=halo_send.at[c, p, 1],
                recv_sem=halo_recv.at[c, p, 1],
                device_id=(tx, left),
                device_id_type=MESH,
            ),
        )

    def points_halo():
        return (
            pltpu.make_async_remote_copy(
                src_ref=p_right,
                dst_ref=p_from_left,
                send_sem=pts_send.at[0],
                recv_sem=pts_recv.at[0],
                device_id=(tx, right),
                device_id_type=MESH,
            ),
            pltpu.make_async_remote_copy(
                src_ref=p_left,
                dst_ref=p_from_right,
                send_sem=pts_send.at[1],
                recv_sem=pts_recv.at[1],
                device_id=(tx, left),
                device_id_type=MESH,
            ),
        )

    def own(h):
        return pltpu.make_async_copy(
            rhs.at[:, :, pl.ds(h * WIDE, WIDE)], mine.at[h, pl.ds(0, leaves)], own_sem.at[h]
        )

    halves = mine.shape[0]

    loads = (
        pltpu.make_async_copy(leaf_inv, inv, load_sem.at[0]),
        pltpu.make_async_copy(coupling.at[0], coup_rows, load_sem.at[1]),
        pltpu.make_async_copy(level_one, lone, load_sem.at[2]),
    )

    for copy in halo(0, 0):
        copy.start()
    for copy in small:
        copy.wait()
    coords = pts[...].astype(F32)

    def two_rows(x):
        return jnp.concatenate([x[:, :half], x[:, half:]], axis=0).astype(BF16)

    p_right[...] = two_rows(coords[:, own_rows - side :])
    p_left[...] = two_rows(coords[:, :side])
    for copy in points_halo():
        copy.start()
    for c in range(chunks):
        for p in range(0 if c else 1, pieces[c]):
            for copy in halo(c, p):
                copy.start()
    for copy in loads:
        copy.start()
    for h in range(halves):
        own(h).start()
        mine[h, leaves] = jnp.zeros((PTS, WIDE), BF16)
    weights[leaves * NBR] = jnp.zeros((PTS, PTS), BF16)

    def tails(x, sign_rows):
        sq = jnp.sum(x * x, axis=0, keepdims=True) * (-0.5 / DIM)
        high = sq.astype(BF16).astype(F32)
        rest = sq - high
        mid = rest.astype(BF16).astype(F32)
        low = rest - mid
        row = lax.broadcasted_iota(jnp.int32, (8, x.shape[1]), 0)
        at = 3 * sign_rows
        parts = jnp.where(
            row == at, high, jnp.where(row == at + 1, mid, jnp.where(row == at + 2, low, 1.0))
        )
        return jnp.where(row < 6, parts, 0.0)

    def put_other(place, x):
        block = jnp.concatenate([x, tails(x, 0)], axis=0).astype(BF16)
        for j in range(x.shape[1] // PTS):
            v_ext[place + j] = block[:, j * PTS : (j + 1) * PTS]

    u_all[...] = jnp.concatenate([coords * (1.0 / DIM), tails(coords, 1)], axis=0)
    put_other(WIN, coords)

    loads[0].wait()

    def leaf_setup(q, _):
        spot = lax.broadcasted_iota(jnp.int32, (PTS, SK), 0)
        for k in range(2):
            i = 2 * q + k
            u_leaf[i] = u_all[:, rows_of(i, PTS)].T.astype(BF16)
            spread = (spot == leaf_skel[pl.ds(i, 1), :]).astype(F32)
            leaf_pick[i] = spread.T.astype(BF16)
            cols = mm(inv[i], spread.astype(BF16)).astype(BF16)
            inv_cols[q, :, k * SK : (k + 1) * SK] = cols
        return 0

    lax.fori_loop(0, leaves // 2, leaf_setup, 0)
    for n in range(nodes):
        spot = lax.broadcasted_iota(jnp.int32, (node_rows, SK), 0)
        spread = (spot == node_skel[pl.ds(n, 1), :]).astype(F32)
        node_spread[n, :, :SK] = spread.astype(BF16)
        node_spread[n, :, SK:] = spread.astype(BF16)
        node_pick[n] = spread.T.astype(BF16)

    for copy in points_halo():
        copy.wait()
    for block, place in ((p_from_left, 0), (p_from_right, WIN + leaves)):
        far = block[...].astype(F32)
        put_other(place, far[:DIM])
        put_other(place + WIN // 2, far[DIM:])

    base = (tx * n_ty + ty) * leaves - WIN

    def place_of(i, s):
        return jnp.clip(neigh[s, i] - base, 0, leaves + 2 * WIN - 1)

    def leaf_kernel(i, _):
        here = u_leaf[i]
        live = counts[i]
        places = [place_of(i, s) for s in range(NBR)]
        first = jnp.where(i < WIN, 0, WIN + leaves)
        for h in range(WIN):
            slot = leaves * NBR
            for s in range(NBR):
                hit = (places[s] == first + h) & (s < live)
                slot = jnp.where(hit, i * NBR + s, slot)
            slot_of[i * WIN + h] = slot
        for s in range(NBR):
            near = jnp.exp2(mm(here, v_ext[places[s]]) * LOG2E)
            weights[i * NBR + s] = jnp.where(s < live, near, 0.0).astype(BF16)
        return 0

    lax.fori_loop(0, leaves, leaf_kernel, 0, unroll=2)

    def own_near(h):
        cols = pl.ds(h * WIDE, WIDE)

        def own_place(i, s):
            at = place_of(i, s) - WIN
            return jnp.where((at >= 0) & (at < leaves), at, leaves)

        def leaf(i, _):
            total = mm(weights[i * NBR], mine[h, own_place(i, 0)])
            for s in range(1, NBR):
                total += mm(weights[i * NBR + s], mine[h, own_place(i, s)])
            out[rows_of(i, PTS), cols] = total
            return 0

        lax.fori_loop(0, leaves, leaf, 0, unroll=8)

    def upward(c):
        cols = pl.ds(starts[c], widths[c])
        h, lane = divmod(starts[c], WIDE)

        def with_halo(i, block, places):
            total = out[rows_of(i, PTS), cols]
            for at in places:
                total += mm(weights[slot_of[i * WIN + at]], block[at])
            return total

        def finish(done, near):
            own_rhs = [mine[h, i, :, lane : lane + widths[c]].astype(F32) for i in done]
            return [(r - t * PTS ** (-0.5)).astype(BF16) for r, t in zip(own_rhs, near)]

        def inverse(done, resid):
            inner = [mm(inv[i], r) for i, r in zip(done, resid)]
            for i, z in zip(done, inner):
                out[rows_of(i, PTS), cols] = z
            for i, z in zip(done, inner):
                up[c][rows_of(i, SK), :] = mm(leaf_pick[i], z.astype(BF16)).astype(BF16)

        for p in range(WIN // 2):
            if c > 0 and p == (0 if c < chunks - 1 else WIN // 2 - 2):
                pass_on(c - 1, hops)
            step = WIN // 2 // pieces[c]
            if p % step == 0:
                for copy in halo(c, p // step):
                    copy.wait()
            low, high = (WIN - 1 - 2 * p, WIN - 2 - 2 * p), (2 * p, 2 * p + 1)

            def leaf(i, _):
                j = leaves - 1 - i
                a = with_halo(i, from_left[c], low)
                b = with_halo(j, from_right[c], high)
                out[rows_of(i, PTS), cols] = a
                out[rows_of(j, PTS), cols] = b
                return 0

            if p < WIN // 2 - 1:
                lax.fori_loop(0, WIN - 2 - 2 * p, leaf, 0, unroll=2)
            done = (WIN - 1 - 2 * p, WIN - 2 - 2 * p, WIN + 2 * p, WIN + 2 * p + 1)
            near = (
                with_halo(done[0], from_left[c], low[:1]),
                with_halo(done[1], from_left[c], low),
                with_halo(done[2], from_right[c], high[:1]),
                with_halo(done[3], from_right[c], high),
            )
            resid = finish(done, near)
            if c == chunks - 1:
                inverse(done, resid)
            else:
                for i, r in zip(done, resid):
                    held[i, :, : widths[c]] = r
        if c < chunks - 1:

            def group(g, _):
                done = [g * 4 + k for k in range(4)]
                inverse(done, [held[i, :, : widths[c]] for i in done])
                return 0

            lax.fori_loop(0, leaves // 4, group, 0, unroll=2)

    def top_copy(c, src, owner, sem, t):
        return pltpu.make_async_remote_copy(
            src_ref=src,
            dst_ref=gath[c].at[rows_of(owner, nodes * SK)],
            send_sem=top_send.at[c, sem],
            recv_sem=top_recv.at[c, sem],
            device_id=(t, ty),
            device_id_type=MESH,
        )

    def far_copy(c, k):
        return top_copy(c, top[c], tx, k, lax.rem(tx + 2 * k, n_tx))

    def near_copy(c):
        return top_copy(c, top[c], tx, 0, mate)

    def second_copy(c, k):
        owner = lax.rem(tx + n_tx - 2 * k, n_tx)
        block = gath[c].at[rows_of(owner, nodes * SK)]
        return top_copy(c, block, owner, turns - 1 + k, mate)

    def send_top(c):
        for n in range(nodes):
            block = mm(node_pick[n], up[c][pl.ds(n * node_rows, node_rows), :]).astype(BF16)
            top[c][pl.ds(n * SK, SK), :] = block
            gath[c][pl.ds(pl.multiple_of(tx * nodes * SK + n * SK, SK), SK), :] = block
        for k in hops:
            far_copy(c, k).start()
        near_copy(c).start()

    def pass_on(c, which):
        for k in which:
            far_copy(c, k).wait_recv()
            second_copy(c, k).start()

    def gathered(c):
        for k in hops:
            far_copy(c, k).wait_send()
        near_copy(c).wait()
        for k in hops:
            second_copy(c, k).wait()

    def correct(c, which):
        cols = pl.ds(starts[c], widths[c])

        def store(i, x):
            rows = pl.ds(i * PTS, PTS)
            out[rows, cols] = out[rows, cols] - x

        downward(which, coup_rows, gath[c], up[c], node_spread, lone, inv_cols, store)

    for h in range(halves):
        own(h).wait()
    for h in range(halves):
        own_near(h)
    last = chunks - 1
    for c in range(chunks):
        upward(c)
        send_top(c)
    loads[1].wait()
    loads[2].wait()
    for c in range(last):
        gathered(c)
    for c in range(last - 1):
        correct(c, range(nodes))
    pass_on(last, hops[:-1])
    for n in range(nodes):
        if n == nodes - 1:
            pass_on(last, hops[-1:])
        correct(last - 1, range(n, n + 1))
    gathered(last)


def last_kernel(nodes, start, held, gath, up, coup_rows, lone, node_spread, inv_cols, out, sol, sem):
    width = held.shape[1] - start
    part = held.shape[0] // (2 * nodes)

    def ready(b):
        here = (pl.ds(b * part, part), pl.ds(0, start))
        return pltpu.make_async_copy(held.at[here], out.at[here], sem.at[0, b])

    def done(b):
        rows = pl.ds(b * part, part)
        return pltpu.make_async_copy(sol.at[rows], out.at[rows, pl.ds(start, width)], sem.at[1, b])

    def store(i, x):
        rows = pl.ds(i * PTS, PTS)
        sol[rows, :] = held[rows, pl.ds(start, width)] - x
        if (i + 1) % (GROUP // 2) == 0:
            done(i // (GROUP // 2)).start()

    for b in range(2 * nodes):
        ready(b).start()
    downward(range(nodes), coup_rows, gath, up, node_spread, lone, inv_cols, store)
    for b in range(2 * nodes):
        ready(b).wait()
        done(b).wait()


def on_device(rhs, pts, leaf_inv, level_one, coupling, neigh, counts, leaf_skel, node_skel):
    rows, cols = rhs.shape
    leaves, nodes = leaf_inv.shape[0], level_one.shape[0]
    n_tx, n_ty = lax.axis_size("tx"), lax.axis_size("ty")
    widths = (WIDE,) * (cols // WIDE - 1) + (WIDE // 2,) * 2
    pieces = (4,) + (1,) * (len(widths) - 2) + (4,)
    chunks = len(widths)
    side = WIN * PTS
    halves = cols // WIDE
    dma = pltpu.SemaphoreType.DMA
    tops = n_tx * nodes * SK
    scratch = (
        [pltpu.VMEM((WIN, PTS, w), BF16) for w in widths * 2]
        + [pltpu.VMEM((nodes * SK, w), BF16) for w in widths]
        + [pltpu.VMEM((leaves * SK, w), BF16) for w in widths[:-1]]
        + [pltpu.VMEM((tops, w), BF16) for w in widths[:-1]]
        + [
            pltpu.VMEM((halves, leaves + 1, PTS, WIDE), BF16),
            pltpu.VMEM((leaves, PTS, WIDE), BF16),
            pltpu.SMEM((leaves * WIN,), jnp.int32),
            pltpu.VMEM((leaves * NBR + 1, PTS, PTS), BF16),
            pltpu.VMEM(leaf_inv.shape, BF16),
            pltpu.VMEM((leaves, SK, PTS), BF16),
            pltpu.VMEM((nodes, SK, GROUP * SK), BF16),
            pltpu.VMEM((2 * DIM, side // 2), BF16),
            pltpu.VMEM((2 * DIM, side // 2), BF16),
            pltpu.VMEM((2 * DIM, side // 2), BF16),
            pltpu.VMEM((2 * DIM, side // 2), BF16),
            pltpu.VMEM((leaves + 2 * WIN, 2 * DIM, PTS), BF16),
            pltpu.VMEM((2 * DIM, rows), F32),
            pltpu.VMEM((leaves, PTS, 2 * DIM), BF16),
            dma((chunks, max(pieces), 2)),
            dma((chunks, max(pieces), 2)),
            dma((2,)),
            dma((2,)),
            dma((chunks, n_tx - 1)),
            dma((chunks, n_tx - 1)),
            dma((halves,)),
            dma((3,)),
            pltpu.VMEM(pts.shape, BF16),
            pltpu.VMEM(leaf_skel.shape, jnp.int32),
            pltpu.VMEM(node_skel.shape, jnp.int32),
            pltpu.SMEM(neigh.shape[::-1], jnp.int32),
            pltpu.SMEM(counts.shape, jnp.int32),
            dma((5,)),
        ]
    )
    vmem = pl.BlockSpec(memory_space=pltpu.VMEM)
    smem = pl.BlockSpec(memory_space=pltpu.SMEM)
    hbm = pl.BlockSpec(memory_space=pltpu.HBM)
    kept = (
        pltpu.VMEM((rows, cols), F32),
        pltpu.VMEM((tops, widths[-1]), BF16),
        pltpu.VMEM((leaves * SK, widths[-1]), BF16),
        pltpu.VMEM(coupling.shape[1:], BF16),
        pltpu.VMEM(level_one.shape, BF16),
        pltpu.VMEM((nodes, GROUP * SK, 2 * SK), BF16),
        pltpu.VMEM((leaves // 2, PTS, 2 * SK), BF16),
    )
    parts = pl.pallas_call(
        functools.partial(device_kernel, (leaves, nodes, widths, pieces, n_tx, n_ty)),
        out_shape=kept,
        in_specs=[hbm, hbm, hbm, hbm, hbm, hbm, hbm, hbm, hbm],
        out_specs=(vmem,) * len(kept),
        scratch_shapes=scratch,
        compiler_params=pltpu.CompilerParams(
            collective_id=0, has_side_effects=True, vmem_limit_bytes=42 * 2**20
        ),
        cost_estimate=pl.CostEstimate(
            flops=2 * 6_500_000_000, bytes_accessed=20_000_000, transcendentals=8_400_000
        ),
    )(
        rhs.reshape(leaves, PTS, cols),
        pts,
        leaf_inv,
        level_one,
        coupling,
        neigh.T,
        counts,
        leaf_skel,
        node_skel,
    )
    return pl.pallas_call(
        functools.partial(last_kernel, nodes, cols - widths[-1]),
        out_shape=jax.ShapeDtypeStruct((rows, cols), F32),
        in_specs=[vmem] * len(kept),
        out_specs=hbm,
        scratch_shapes=[
            pltpu.VMEM((rows, widths[-1]), F32),
            dma((2, 2 * nodes)),
        ],
        compiler_params=pltpu.CompilerParams(vmem_limit_bytes=16 * 2**20),
        cost_estimate=pl.CostEstimate(
            flops=2 * 250_000_000, bytes_accessed=8_400_000, transcendentals=0
        ),
    )(*parts)


def solution(mesh):
    return jax.shard_map(
        on_device,
        mesh=mesh,
        in_specs=(
            P(("tx", "ty"), None),
            P(None, ("tx", "ty")),
            P(("tx", "ty"), None, None),
            P(("tx", "ty"), None, None),
            P("ty", "tx", None),
            P(("tx", "ty"), None),
            P(("tx", "ty")),
            P(("tx", "ty"), None),
            P(("tx", "ty"), None),
        ),
        out_specs=P(("tx", "ty"), None),
        check_vma=False,
    )
```
